128 devices in a mesh: row: 16 (over x_hi, y, core), col: 8 (over x_lo, z).
Axes of the slice: x: 4 (x_hi: 2, x_lo: 2; x = x_hi * 2 + x_lo), y: 4, z: 4, core: 2. Of those that a mesh axis runs over, the one named last changes fastest.
Arguments:
- multispectral: float32 [8, 512, 1024], P('col', 'row'), may hold values from -6 to 6
- panchromatic: float32 [2048, 4096], P('row', 'col'), may hold values from -6 to 6
- band_gains: float32 [8, 3], replicated, may hold values from 0.5 to 2
Outputs:
- sharpened: float32 [8, 2048, 4096], P(None, 'row', 'col')
The draws below stay inside these ranges and needn't reach their ends.
All inputs are finite; a program needn't handle non-finite values.
Results may differ from the reference program's by a relative error of at most 0.000065.
Values sent between devices are 32-bit elements; how exact they have to be, the bound alone decides.
A program may use at most 128 MiB of HBM per device.

```python
import math
import jax
import jax.numpy as jnp
from jax import lax

BANDS = 8
LEVELS = 3
IMG_ROWS = 2048
IMG_COLS = 4096
LOW_ROWS = 512
LOW_COLS = 1024


def levels(own_key, shape, split, smallest, high):
    level = 1.0
    for axis_at, shards_of in split:
        draws = jax.random.uniform(jax.random.fold_in(jax.random.fold_in(own_key, 6), axis_at), (shards_of,), jnp.float32, smallest / len(split), high / len(split))
        level = level * jnp.repeat(jnp.exp(draws), shape[axis_at] // shards_of).reshape((-1,) + (1,) * (len(shape) - 1 - axis_at))
    return level


def gaussian(own_key, extent, width, reach, split=(), held_as=jnp.bfloat16):
    entries = width * jax.random.normal(own_key, extent, jnp.float32)
    if split:
        entries = entries * levels(own_key, extent, split, -0.22, 0.18)
    return jnp.clip(entries, -reach, reach).astype(held_as)


def setup_inputs(seed: int = 0) -> dict:
    keys = jax.random.split(jax.random.key(seed), 4)
    return {
        "multispectral": gaussian(keys[0], (BANDS, LOW_ROWS, LOW_COLS), 1.0, 6.0, ((0, 8), (1, 16)), jnp.float32),
        "panchromatic": gaussian(keys[1], (IMG_ROWS, IMG_COLS), 1.0, 6.0, ((0, 16), (1, 8)), jnp.float32),
        "band_gains": jnp.clip(jnp.exp(jax.random.uniform(keys[2], (BANDS, LEVELS), jnp.float32, math.log(0.5), math.log(2.0))), 0.5, 2.0),
    }


daubechies_taps = [0.2303778133088964, 0.7148465705529154, 0.6308807679298587, -0.0279837694168599, -0.1870348117190931, 0.0308413818355607, 0.0328830116668852, -0.0105974017850690]


def tree_filters(tree_index):
    lowpass = list(daubechies_taps) if tree_index == 0 else list(reversed(daubechies_taps))
    highpass = [((-1) ** tap_index) * lowpass[7 - tap_index] for tap_index in range(8)]
    return lowpass, highpass, 3 + tree_index


def cubic_weight(distance):
    magnitude = abs(distance)
    if magnitude <= 1.0:
        return 1.5 * magnitude ** 3 - 2.5 * magnitude ** 2 + 1.0
    if magnitude < 2.0:
        return -0.5 * magnitude ** 3 + 2.5 * magnitude ** 2 - 4.0 * magnitude + 2.0
    return 0.0


def alternate(phase_parts, axis_dim):
    stacked = jnp.stack(phase_parts, axis=axis_dim + 1)
    new_shape = list(phase_parts[0].shape)
    new_shape[axis_dim] = new_shape[axis_dim] * len(phase_parts)
    return stacked.reshape(new_shape)


def upsample_axis(extended, margin, axis_dim):
    out_count = extended.shape[axis_dim] - 4
    phase_parts = []
    for phase_index in range(4):
        position = (phase_index + 0.5) / 4.0 - 0.5
        floor_shift = math.floor(position)
        fraction = position - floor_shift
        summed = None
        for neighbour in (-1, 0, 1, 2):
            first_index = 2 + floor_shift + neighbour
            strided = lax.slice_in_dim(extended, first_index, first_index + out_count, 1, axis_dim)
            term = cubic_weight(fraction - neighbour) * strided
            summed = term if summed is None else summed + term
        phase_parts.append(summed)
    return alternate(phase_parts, axis_dim)


def upsample_tile(extended, margin):
    return upsample_axis(upsample_axis(extended, margin, 1), margin, 2)


def analyze_axis(extended, tap_sets, offset, axis_dim):
    out_count = (extended.shape[axis_dim] - 8) // 2
    results = []
    for tap_weights in tap_sets:
        summed = None
        for tap_index in range(8):
            first_index = 4 - offset + tap_index
            strided = lax.slice_in_dim(extended, first_index, first_index + 2 * out_count - 1, 2, axis_dim)
            term = tap_weights[tap_index] * strided
            summed = term if summed is None else summed + term
        results.append(summed)
    return results


def synthesize_axis(low_ext, high_ext, lowpass, highpass, offset, axis_dim):
    present = [(member, tap_weights) for member, tap_weights in ((low_ext, lowpass), (high_ext, highpass)) if member is not None]
    if len(present) == 0:
        return None
    out_count = present[0][0].shape[axis_dim] - 4
    phase_parts = []
    for parity in (0, 1):
        summed = None
        for member, tap_weights in present:
            for tap_index in range(8):
                if (offset + parity - tap_index) % 2 == 0:
                    first_index = 2 + (offset + parity - tap_index) // 2
                    strided = lax.slice_in_dim(member, first_index, first_index + out_count, 1, axis_dim)
                    term = tap_weights[tap_index] * strided
                    summed = term if summed is None else summed + term
        phase_parts.append(summed)
    return alternate(phase_parts, axis_dim)


def rows_full(col_low, col_high, row_tree):
    lowpass, highpass, offset = tree_filters(row_tree)
    low_low, low_high = analyze_axis(col_low, [lowpass, highpass], offset, 1)
    high_low, high_high = analyze_axis(col_high, [lowpass, highpass], offset, 1)
    return low_low, (low_high, high_low, high_high)


def analyze_full(extended, col_tree, row_tree):
    lowpass, highpass, offset = tree_filters(col_tree)
    col_low, col_high = analyze_axis(extended, [lowpass, highpass], offset, 2)
    return rows_full(col_low, col_high, row_tree)


def analyze_low(extended, col_tree, row_tree):
    col_lowpass, col_highpass, col_offset = tree_filters(col_tree)
    row_lowpass, row_highpass, row_offset = tree_filters(row_tree)
    col_low = analyze_axis(extended, [col_lowpass], col_offset, 2)[0]
    return analyze_axis(col_low, [row_lowpass], row_offset, 1)[0]


def synthesize_tile(low_low, low_high, high_low, high_high, col_tree, row_tree):
    col_lowpass, col_highpass, col_offset = tree_filters(col_tree)
    row_lowpass, row_highpass, row_offset = tree_filters(row_tree)
    col_low = synthesize_axis(low_low, low_high, row_lowpass, row_highpass, row_offset, 1)
    col_high = synthesize_axis(high_low, high_high, row_lowpass, row_highpass, row_offset, 1)
    return synthesize_axis(col_low, col_high, col_lowpass, col_highpass, col_offset, 2)


def wrap_pad(field_stack, rim_width):
    return jnp.pad(field_stack, ((0, 0), (rim_width, rim_width), (rim_width, rim_width)), mode="wrap")


def reference(multispectral, panchromatic, band_gains):
    upsampled = upsample_tile(wrap_pad(multispectral, 2), 2)
    accumulated = jnp.zeros(upsampled.shape, jnp.float32)
    for col_tree in range(2):
        for row_tree in range(2):
            pan_low = panchromatic[None]
            pan_details = []
            for level_index in range(LEVELS):
                pan_low, details = analyze_full(wrap_pad(pan_low, 4), col_tree, row_tree)
                pan_details.append(details)

            def one_band(operands):
                band_field, gains_row = operands
                current = band_field[None]
                for level_index in range(LEVELS):
                    current = analyze_low(wrap_pad(current, 4), col_tree, row_tree)
                for level_index in reversed(range(LEVELS)):
                    merged_bands = [gains_row[level_index] * detail for detail in pan_details[level_index]]
                    padded = [wrap_pad(member, 2) for member in [current] + merged_bands]
                    current = synthesize_tile(padded[0], padded[1], padded[2], padded[3], col_tree, row_tree)
                return current[0]

            accumulated = accumulated + lax.map(one_band, (upsampled, band_gains))
    return 0.25 * accumulated
```

```python
import functools
import math

import jax
import jax.numpy as jnp
import ml_dtypes
import numpy as np
from jax import lax
from jax.experimental import pallas as pl
from jax.experimental.pallas import tpu as pltpu
from jax.sharding import PartitionSpec as P

MESH = pl.DeviceIdType.MESH
BF16 = ml_dtypes.bfloat16

TAPS = [
    0.2303778133088964,
    0.7148465705529154,
    0.6308807679298587,
    -0.0279837694168599,
    -0.1870348117190931,
    0.0308413818355607,
    0.0328830116668852,
    -0.0105974017850690,
]

ROWS, COLS = 128, 512
LROWS, LCOLS = 32, 128
PAN_RIM = 48
PAN_EXT = ROWS + 2 * PAN_RIM
MS_RIM = 16
BANDS = 8


def projection(level):
    step = 2**level
    rows = [{} for _ in range(8)]
    for tree in range(2):
        taps = TAPS if tree == 0 else TAPS[::-1]
        cascade, shift = [1.0], 0
        for lev in range(level):
            longer = [0.0] * (len(cascade) + 7 * 2**lev)
            for i, value in enumerate(cascade):
                for j, tap in enumerate(taps):
                    longer[i + j * 2**lev] += value * tap
            cascade, shift = longer, shift + (3 + tree) * 2**lev
        span = len(cascade)
        for m in range(8):
            for k in range(-64, 64):
                at = m - step * k + shift
                if 0 <= at < span:
                    for i, value in enumerate(cascade):
                        offset = step * k - shift + i - m
                        rows[m][offset] = rows[m].get(offset, 0.0) + 0.5 * cascade[at] * value
    return rows


def cubic_weight(distance):
    magnitude = abs(distance)
    if magnitude <= 1.0:
        return 1.5 * magnitude**3 - 2.5 * magnitude**2 + 1.0
    if magnitude < 2.0:
        return -0.5 * magnitude**3 + 2.5 * magnitude**2 - 4.0 * magnitude + 2.0
    return 0.0


def upsampled_projection():
    rows = [{} for _ in range(8)]
    for m, weights in enumerate(projection(3)):
        for offset in sorted(weights):
            position = (m + offset + 0.5) / 4.0 - 0.5
            floor = math.floor(position)
            for low in range(floor - 1, floor + 3):
                term = weights[offset] * cubic_weight(position - low)
                rows[m][low] = rows[m].get(low, 0.0) + term
    return rows


def split_parts(matrix):
    high = matrix.astype(np.float32).astype(BF16)
    low = (matrix - high.astype(np.float64)).astype(np.float32).astype(BF16)
    return high, low


def pan_matrix(level, outs, ins, start):
    matrix = np.zeros((outs, ins))
    rows = projection(level)
    for m in range(outs):
        for offset, weight in rows[m % 8].items():
            matrix[m, m + offset - start] = weight
    return matrix


def ms_matrix(outs, lows):
    place = {low: at for at, low in lows}
    matrix = np.zeros((outs, max(at for at, _ in lows) + 1))
    rows = upsampled_projection()
    for m in range(outs):
        for low, weight in rows[m % 8].items():
            matrix[m, place[low + 2 * (m // 8)]] = weight
    return matrix


def make_tables():
    high, low = split_parts(ms_matrix(ROWS, [(i, i - MS_RIM) for i in range(LROWS + 2 * MS_RIM)]))
    ms_rows = np.concatenate([high, high, low], 1)
    lows = [(i, i) for i in range(LCOLS)]
    lows += [(LCOLS + i, i - MS_RIM) for i in range(MS_RIM)]
    lows += [(LCOLS + MS_RIM + i, LCOLS + i) for i in range(MS_RIM)]
    matrix = ms_matrix(COLS, lows)
    matrix = np.pad(matrix, ((0, 0), (0, 256 - matrix.shape[1]))).T
    high, low = split_parts(matrix)
    ms_cols = np.concatenate([high, high, low], 0)
    matrix = np.concatenate([pan_matrix(level, 128, 256, -64) for level in (1, 2, 3)], 0).T
    high, low = split_parts(matrix)
    pan_cols = np.concatenate([high, high, low], 0)
    pan_rows = []
    for level in (1, 2, 3):
        high, low = split_parts(pan_matrix(level, ROWS, PAN_EXT, -PAN_RIM))
        pan_rows.append(np.concatenate([high, high, low], 1))
    return ms_rows, ms_cols, pan_cols, np.stack(pan_rows)


def parts_of(x):
    high = x.astype(jnp.bfloat16)
    low = (x - high.astype(jnp.float32)).astype(jnp.bfloat16)
    return high, low


def kernel(
    nr, nc,
    ms_hbm, pan_hbm, gains, ms_rows_hbm, ms_cols_hbm, pan_cols_hbm, pan_rows_hbm,
    out_ref,
    ms_own, stage, mbuf, pan_ext, pstage, precv,
    ms_rows, ms_cols, pan_cols, pan_rows,
    pan_split, zbuf, qbuf, xsplit, ybuf,
    load_sems, own_sem, ms_send, ms_recv, pan_send, pan_recv,
):
    r, c = lax.axis_index("row"), lax.axis_index("col")
    row_of = {d: lax.rem(r + d + nr, nr) for d in (-1, 0, 1)}
    col_of = [lax.rem(c + k, nc) for k in range(nc)]

    barrier = pltpu.get_barrier_semaphore()
    for d in (-1, 0, 1):
        for k in range(nc):
            if d or k:
                pl.semaphore_signal(
                    barrier, inc=1, device_id=(row_of[d], col_of[k]), device_id_type=MESH
                )

    ms_load = pltpu.make_async_copy(ms_hbm.at[0], ms_own, load_sems.at[0])
    pan_load = pltpu.make_async_copy(
        pan_hbm, pan_ext.at[PAN_RIM : PAN_RIM + ROWS], load_sems.at[1]
    )
    table_loads = [
        pltpu.make_async_copy(source, target, load_sems.at[2 + i])
        for i, (source, target) in enumerate(
            (
                (pan_cols_hbm, pan_cols),
                (pan_rows_hbm, pan_rows),
                (ms_cols_hbm, ms_cols),
                (ms_rows_hbm, ms_rows),
            )
        )
    ]
    ms_load.start()
    pan_load.start()
    for load in table_loads:
        load.start()

    lane = lax.broadcasted_iota(jnp.int32, (8, 128), 1)

    ms_load.wait()
    for dest in range(nc):
        tile = slice(128 * dest, 128 * dest + 128)
        before = (dest - 1) % nc
        after = (dest + 1) % nc
        stage[dest, 0:16] = ms_own[0:16, tile]
        stage[dest, 24:40] = ms_own[16:32, tile]
        rim = None
        for q in range(4):
            rows = slice(8 * q, 8 * q + 8)
            both = jnp.where(
                lane < 64,
                ms_own[rows, 128 * after : 128 * after + 128],
                ms_own[rows, 128 * before : 128 * before + 128],
            )
            both = pltpu.roll(both, (16 + 32 * q) % 128, 1)
            rim = both if rim is None else jnp.where(lane < 32 * q, rim, both)
        stage[dest, 16:24] = rim

    pan_load.wait()
    for at, (first, count) in ((0, (0, 64)), (64, (80, 24)), (88, (0, 24))):
        for step in range(0, count, 8):
            upper = PAN_RIM + first + step
            lower = upper + count
            for side, column in ((0, 384), (1, 0)):
                one = pan_ext[upper : upper + 8, column : column + 128]
                two = pan_ext[lower : lower + 8, column : column + 128]
                if side == 0:
                    packed = jnp.where(lane < 64, pltpu.roll(one, 64, 1), two)
                else:
                    packed = jnp.where(lane < 64, one, pltpu.roll(two, 64, 1))
                pstage[side, at + step : at + step + 8] = packed

    pl.semaphore_wait(barrier, 3 * nc - 1)

    def remote(source, target, send_sem, recv_sem, d, k):
        return pltpu.make_async_remote_copy(
            src_ref=source,
            dst_ref=target,
            send_sem=send_sem,
            recv_sem=recv_sem,
            device_id=(row_of[d], col_of[k % nc]),
            device_id_type=MESH,
        )

    pan_copies = []
    own = PAN_RIM
    for d, source, target in (
        (1, pan_ext.at[own + ROWS - PAN_RIM : own + ROWS], pan_ext.at[0:PAN_RIM]),
        (-1, pan_ext.at[own : own + PAN_RIM], pan_ext.at[own + ROWS : PAN_EXT]),
    ):
        at = len(pan_copies)
        pan_copies.append(remote(source, target, pan_send.at[at], pan_recv.at[at], d, 0))
    for side, k in ((0, 1), (1, -1)):
        for d, rows in ((0, slice(0, 64)), (1, slice(64, 88)), (-1, slice(88, 112))):
            at = len(pan_copies)
            pan_copies.append(
                remote(
                    pstage.at[side, rows], precv.at[side, rows],
                    pan_send.at[at], pan_recv.at[at], d, k,
                )
            )
    ms_copies = []
    spans = {0: (slice(0, 40), slice(24, 64)), 1: (slice(16, 40), slice(0, 24)), -1: (slice(0, 24), slice(64, 88))}
    for d in (0, 1, -1):
        source, target = spans[d]
        for k in range(nc):
            if d or k:
                ms_copies.append(
                    remote(
                        stage.at[col_of[k], source], mbuf.at[c, target],
                        ms_send.at[d + 1, k], ms_recv.at[d + 1, c], d, k,
                    )
                )
    own_copy = pltpu.make_async_copy(stage.at[c], mbuf.at[c, 24:64], own_sem)
    for copy in pan_copies + ms_copies:
        copy.start()
    own_copy.start()

    for copy in pan_copies:
        copy.wait_recv()
    for step in range(0, PAN_EXT, 8):
        rows = slice(step, step + 8)
        if step < 48:
            base, at, half = 0, 64, 24
        elif step < 176:
            base, at, half = 48, 0, 64
        else:
            base, at, half = 176, 88, 24
        second = step - base >= half
        inside = step - base - (half if second else 0)
        left = precv[0, at + inside : at + inside + 8]
        right = precv[1, at + inside : at + inside + 8]
        if second:
            left = pltpu.roll(left, 64, 1)
        else:
            right = pltpu.roll(right, 64, 1)
        tiles = [left]
        tiles += [pltpu.roll(pan_ext[rows, 128 * t : 128 * t + 128], 64, 1) for t in range(4)]
        tiles += [right]
        for t in range(5):
            value = jnp.where(lane < 64, tiles[t], tiles[t + 1])
            high, low = parts_of(value)
            pan_split[0, rows, 128 * t : 128 * t + 128] = high.astype(jnp.float32)
            pan_split[1, rows, 128 * t : 128 * t + 128] = low.astype(jnp.float32)

    for load in table_loads:
        load.wait()
    for j in range(4):
        window = slice(128 * j, 128 * j + 256)
        high = pan_split[0, :, window].astype(jnp.bfloat16)
        low = pan_split[1, :, window].astype(jnp.bfloat16)
        z = jnp.dot(
            jnp.concatenate([high, low, high], 1), pan_cols[...], preferred_element_type=jnp.float32
        )
        for level in range(3):
            high, low = parts_of(z[:, 128 * level : 128 * level + 128])
            for at, part in ((0, high), (1, low), (2, high)):
                zbuf[level, PAN_EXT * at : PAN_EXT * (at + 1), 128 * j : 128 * j + 128] = part
    for level in range(3):
        qbuf[level] = jnp.dot(pan_rows[level], zbuf[level], preferred_element_type=jnp.float32)

    own_copy.wait()
    for d in (-1, 0, 1):
        source, target = spans[d]
        for k in range(nc):
            if d or k:
                remote(
                    stage.at[col_of[k], source], mbuf.at[col_of[k], target],
                    ms_send.at[d + 1, k], ms_recv.at[1 - d if d else 1, col_of[k]], d, k,
                ).wait_recv()

    def gather_band(b, carry):
        for g, (main, rim, q) in enumerate(
            (
                (8, 0, 2), (16, 0, 3),
                (24, 40, 0), (32, 40, 1), (48, 40, 2), (56, 40, 3),
                (64, 80, 0), (72, 80, 1),
            )
        ):
            rows = pl.ds(pl.multiple_of(64 * b, 64) + 8 * g, 8)
            edge = mbuf[b, rim : rim + 8]
            if q:
                edge = pltpu.roll(edge, 128 - 32 * q, 1)
            xsplit[rows, 0:128] = mbuf[b, main : main + 8]
            xsplit[rows, 128:256] = edge
        return carry

    lax.fori_loop(0, BANDS, gather_band, 0)
    high, low = parts_of(xsplit[...])
    ybuf[...] = jnp.dot(
        jnp.concatenate([high, low, high], 1), ms_cols[...], preferred_element_type=jnp.float32
    )

    def finish_band(b, carry):
        g1, g2, g3 = gains[0, b], gains[1, b], gains[2, b]
        high, low = parts_of(ybuf[pl.ds(pl.multiple_of(64 * b, 64), 64)])
        total = jnp.dot(
            ms_rows[...], jnp.concatenate([high, low, high], 0), preferred_element_type=jnp.float32
        )
        total += g1 * pan_ext[PAN_RIM : PAN_RIM + ROWS]
        total += (g2 - g1) * qbuf[0] + (g3 - g2) * qbuf[1] - g3 * qbuf[2]
        out_ref[b] = total
        return carry

    lax.fori_loop(0, BANDS, finish_band, 0)

    for copy in pan_copies + ms_copies:
        copy.wait_send()


def on_device(nr, nc, tables, ms, pan, gains):
    f32 = jnp.float32
    bf16 = jnp.bfloat16
    hbm = pl.BlockSpec(memory_space=pl.ANY)
    return pl.pallas_call(
        functools.partial(kernel, nr, nc),
        out_shape=jax.ShapeDtypeStruct((BANDS, ROWS, COLS), f32),
        in_specs=[hbm, hbm, pl.BlockSpec(memory_space=pltpu.SMEM)] + [hbm] * 4,
        out_specs=pl.BlockSpec(memory_space=pltpu.VMEM),
        scratch_shapes=[
            pltpu.VMEM((LROWS, nc * LCOLS), f32),
            pltpu.VMEM((nc, 40, 128), f32),
            pltpu.VMEM((BANDS, 88, 128), f32),
            pltpu.VMEM((PAN_EXT, COLS), f32),
            pltpu.VMEM((2, 112, 128), f32),
            pltpu.VMEM((2, 112, 128), f32),
            *[pltpu.VMEM(table.shape, bf16) for table in tables],
            pltpu.VMEM((2, PAN_EXT, COLS + 128), f32),
            pltpu.VMEM((3, 3 * PAN_EXT, COLS), bf16),
            pltpu.VMEM((3, ROWS, COLS), f32),
            pltpu.VMEM((BANDS * 64, 256), f32),
            pltpu.VMEM((BANDS * 64, COLS), f32),
            pltpu.SemaphoreType.DMA((6,)),
            pltpu.SemaphoreType.DMA,
            pltpu.SemaphoreType.DMA((3, nc)),
            pltpu.SemaphoreType.DMA((3, nc)),
            pltpu.SemaphoreType.DMA((8,)),
            pltpu.SemaphoreType.DMA((8,)),
        ],
        compiler_params=pltpu.CompilerParams(
            collective_id=0, has_side_effects=True, vmem_limit_bytes=32 * 1024 * 1024
        ),
    )(ms, pan, gains.T, *[jnp.asarray(table) for table in tables])


def solution(mesh):
    tables = make_tables()
    nr, nc = mesh.shape["row"], mesh.shape["col"]
    return jax.shard_map(
        functools.partial(on_device, nr, nc, tables),
        mesh=mesh,
        in_specs=(P("col", "row", None), P("row", "col"), P()),
        out_specs=P(None, "row", "col"),
        check_vma=False,
    )
```

```python
import functools
import math

import jax
import jax.numpy as jnp
import ml_dtypes
import numpy as np
from jax import lax
from jax.experimental import pallas as pl
from jax.experimental.pallas import tpu as pltpu
from jax.sharding import PartitionSpec as P

MESH = pl.DeviceIdType.MESH
BF16 = ml_dtypes.bfloat16

TAPS = [
    0.2303778133088964,
    0.7148465705529154,
    0.6308807679298587,
    -0.0279837694168599,
    -0.1870348117190931,
    0.0308413818355607,
    0.0328830116668852,
    -0.0105974017850690,
]

ROWS, COLS = 128, 512
LROWS, LCOLS = 32, 128
PAN_RIM = 48
PAN_EXT = ROWS + 2 * PAN_RIM
MS_RIM = 16
BANDS = 8


def projection(level):
    step = 2**level
    rows = [{} for _ in range(8)]
    for tree in range(2):
        taps = TAPS if tree == 0 else TAPS[::-1]
        cascade, shift = [1.0], 0
        for lev in range(level):
            longer = [0.0] * (len(cascade) + 7 * 2**lev)
            for i, value in enumerate(cascade):
                for j, tap in enumerate(taps):
                    longer[i + j * 2**lev] += value * tap
            cascade, shift = longer, shift + (3 + tree) * 2**lev
        span = len(cascade)
        for m in range(8):
            for k in range(-64, 64):
                at = m - step * k + shift
                if 0 <= at < span:
                    for i, value in enumerate(cascade):
                        offset = step * k - shift + i - m
                        rows[m][offset] = rows[m].get(offset, 0.0) + 0.5 * cascade[at] * value
    return rows


def cubic_weight(distance):
    magnitude = abs(distance)
    if magnitude <= 1.0:
        return 1.5 * magnitude**3 - 2.5 * magnitude**2 + 1.0
    if magnitude < 2.0:
        return -0.5 * magnitude**3 + 2.5 * magnitude**2 - 4.0 * magnitude + 2.0
    return 0.0


def upsampled_projection():
    rows = [{} for _ in range(8)]
    for m, weights in enumerate(projection(3)):
        for offset in sorted(weights):
            position = (m + offset + 0.5) / 4.0 - 0.5
            floor = math.floor(position)
            for low in range(floor - 1, floor + 3):
                term = weights[offset] * cubic_weight(position - low)
                rows[m][low] = rows[m].get(low, 0.0) + term
    return rows


def split_parts(matrix):
    high = matrix.astype(np.float32).astype(BF16)
    low = (matrix - high.astype(np.float64)).astype(np.float32).astype(BF16)
    return high, low


def pan_matrix(level, outs, ins, start):
    matrix = np.zeros((outs, ins))
    rows = projection(level)
    for m in range(outs):
        for offset, weight in rows[m % 8].items():
            matrix[m, m + offset - start] = weight
    return matrix


def ms_matrix(outs, lows):
    place = {low: at for at, low in lows}
    matrix = np.zeros((outs, max(at for at, _ in lows) + 1))
    rows = upsampled_projection()
    for m in range(outs):
        for low, weight in rows[m % 8].items():
            matrix[m, place[low + 2 * (m // 8)]] = weight
    return matrix


def make_tables():
    high, low = split_parts(ms_matrix(ROWS, [(i, i - MS_RIM) for i in range(LROWS + 2 * MS_RIM)]))
    ms_rows = np.concatenate([high, high, low], 1)
    lows = [(i, i) for i in range(LCOLS)]
    lows += [(LCOLS + i, i - MS_RIM) for i in range(MS_RIM)]
    lows += [(LCOLS + MS_RIM + i, LCOLS + i) for i in range(MS_RIM)]
    matrix = ms_matrix(COLS, lows)
    matrix = np.pad(matrix, ((0, 0), (0, 256 - matrix.shape[1]))).T
    high, low = split_parts(matrix)
    ms_cols = np.concatenate([high, high, low], 0)
    matrix = np.concatenate([pan_matrix(level, 128, 256, -64) for level in (1, 2, 3)], 0).T
    high, low = split_parts(matrix)
    pan_cols = np.concatenate([high, high, low], 0)
    pan_rows = []
    for level in (1, 2, 3):
        high, low = split_parts(pan_matrix(level, ROWS, PAN_EXT, -PAN_RIM))
        pan_rows.append(np.concatenate([high, high, low], 1))
    return ms_rows, ms_cols, pan_cols, np.stack(pan_rows)


def parts_of(x):
    high = x.astype(jnp.bfloat16)
    low = (x - high.astype(jnp.float32)).astype(jnp.bfloat16)
    return high, low


def kernel(
    nr, nc,
    ms_hbm, pan_hbm, gains_hbm, ms_rows_hbm, ms_cols_hbm, pan_cols_hbm, pan_rows_hbm,
    out_ref,
    ms_own, stage, mbuf, pan_ext, pstage, precv,
    ms_rows, ms_cols, pan_cols, pan_rows,
    pan_split, zbuf, qbuf, xsplit, ybuf,
    gains, load_sems, own_sem, ms_send, ms_recv, pan_send, pan_recv,
):
    r, c = lax.axis_index("row"), lax.axis_index("col")
    row_of = {d: lax.rem(r + d + nr, nr) for d in (-1, 0, 1)}
    col_of = [lax.rem(c + k, nc) for k in range(nc)]

    barrier = pltpu.get_barrier_semaphore()
    for d in (-1, 0, 1):
        for k in range(nc):
            if d or k:
                pl.semaphore_signal(
                    barrier, inc=1, device_id=(row_of[d], col_of[k]), device_id_type=MESH
                )

    ms_load = pltpu.make_async_copy(ms_hbm.at[0], ms_own, load_sems.at[0])
    pan_load = pltpu.make_async_copy(
        pan_hbm, pan_ext.at[PAN_RIM : PAN_RIM + ROWS], load_sems.at[1]
    )
    table_loads = [
        pltpu.make_async_copy(source, target, load_sems.at[2 + i])
        for i, (source, target) in enumerate(
            (
                (pan_cols_hbm, pan_cols),
                (pan_rows_hbm, pan_rows),
                (ms_cols_hbm, ms_cols),
                (ms_rows_hbm, ms_rows),
                (gains_hbm, gains),
            )
        )
    ]
    ms_load.start()
    pan_load.start()
    for load in table_loads:
        load.start()

    lane = lax.broadcasted_iota(jnp.int32, (8, 128), 1)

    ms_load.wait()
    for dest in range(nc):
        tile = slice(128 * dest, 128 * dest + 128)
        before = (dest - 1) % nc
        after = (dest + 1) % nc
        stage[dest, 0:16] = ms_own[0:16, tile]
        stage[dest, 24:40] = ms_own[16:32, tile]
        rim = None
        for q in range(4):
            rows = slice(8 * q, 8 * q + 8)
            both = jnp.where(
                lane < 64,
                ms_own[rows, 128 * after : 128 * after + 128],
                ms_own[rows, 128 * before : 128 * before + 128],
            )
            both = pltpu.roll(both, (16 + 32 * q) % 128, 1)
            rim = both if rim is None else jnp.where(lane < 32 * q, rim, both)
        stage[dest, 16:24] = rim

    pan_load.wait()
    for at, (first, count) in ((0, (0, 64)), (64, (80, 24)), (88, (0, 24))):
        for step in range(0, count, 8):
            upper = PAN_RIM + first + step
            lower = upper + count
            for side, column in ((0, 384), (1, 0)):
                one = pan_ext[upper : upper + 8, column : column + 128]
                two = pan_ext[lower : lower + 8, column : column + 128]
                if side == 0:
                    packed = jnp.where(lane < 64, pltpu.roll(one, 64, 1), two)
                else:
                    packed = jnp.where(lane < 64, one, pltpu.roll(two, 64, 1))
                pstage[side, at + step : at + step + 8] = packed

    pl.semaphore_wait(barrier, 3 * nc - 1)

    def remote(source, target, send_sem, recv_sem, d, k):
        return pltpu.make_async_remote_copy(
            src_ref=source,
            dst_ref=target,
            send_sem=send_sem,
            recv_sem=recv_sem,
            device_id=(row_of[d], col_of[k % nc]),
            device_id_type=MESH,
        )

    pan_copies = []
    own = PAN_RIM
    for d, source, target in (
        (1, pan_ext.at[own + ROWS - PAN_RIM : own + ROWS], pan_ext.at[0:PAN_RIM]),
        (-1, pan_ext.at[own : own + PAN_RIM], pan_ext.at[own + ROWS : PAN_EXT]),
    ):
        at = len(pan_copies)
        pan_copies.append(remote(source, target, pan_send.at[at], pan_recv.at[at], d, 0))
    for side, k in ((0, 1), (1, -1)):
        for d, rows in ((0, slice(0, 64)), (1, slice(64, 88)), (-1, slice(88, 112))):
            at = len(pan_copies)
            pan_copies.append(
                remote(
                    pstage.at[side, rows], precv.at[side, rows],
                    pan_send.at[at], pan_recv.at[at], d, k,
                )
            )
    ms_copies = []
    spans = {0: (slice(0, 40), slice(24, 64)), 1: (slice(16, 40), slice(0, 24)), -1: (slice(0, 24), slice(64, 88))}
    for d in (0, 1, -1):
        source, target = spans[d]
        for k in range(nc):
            if d or k:
                ms_copies.append(
                    remote(
                        stage.at[col_of[k], source], mbuf.at[c, target],
                        ms_send.at[d + 1, k], ms_recv.at[d + 1, c], d, k,
                    )
                )
    own_copy = pltpu.make_async_copy(stage.at[c], mbuf.at[c, 24:64], own_sem)
    for copy in pan_copies + ms_copies:
        copy.start()
    own_copy.start()

    for copy in pan_copies:
        copy.wait_recv()
    for step in range(0, PAN_EXT, 8):
        rows = slice(step, step + 8)
        if step < 48:
            base, at, half = 0, 64, 24
        elif step < 176:
            base, at, half = 48, 0, 64
        else:
            base, at, half = 176, 88, 24
        second = step - base >= half
        inside = step - base - (half if second else 0)
        left = precv[0, at + inside : at + inside + 8]
        right = precv[1, at + inside : at + inside + 8]
        if second:
            left = pltpu.roll(left, 64, 1)
        else:
            right = pltpu.roll(right, 64, 1)
        tiles = [left]
        tiles += [pltpu.roll(pan_ext[rows, 128 * t : 128 * t + 128], 64, 1) for t in range(4)]
        tiles += [right]
        for t in range(5):
            value = jnp.where(lane < 64, tiles[t], tiles[t + 1])
            high, low = parts_of(value)
            pan_split[0, rows, 128 * t : 128 * t + 128] = high.astype(jnp.float32)
            pan_split[1, rows, 128 * t : 128 * t + 128] = low.astype(jnp.float32)

    for load in table_loads:
        load.wait()
    for j in range(4):
        window = slice(128 * j, 128 * j + 256)
        high = pan_split[0, :, window].astype(jnp.bfloat16)
        low = pan_split[1, :, window].astype(jnp.bfloat16)
        z = jnp.dot(
            jnp.concatenate([high, low, high], 1), pan_cols[...], preferred_element_type=jnp.float32
        )
        for level in range(3):
            high, low = parts_of(z[:, 128 * level : 128 * level + 128])
            for at, part in ((0, high), (1, low), (2, high)):
                zbuf[level, PAN_EXT * at : PAN_EXT * (at + 1), 128 * j : 128 * j + 128] = part
    for level in range(3):
        qbuf[level] = jnp.dot(pan_rows[level], zbuf[level], preferred_element_type=jnp.float32)

    own_copy.wait()
    for d in (-1, 0, 1):
        source, target = spans[d]
        for k in range(nc):
            if d or k:
                remote(
                    stage.at[col_of[k], source], mbuf.at[col_of[k], target],
                    ms_send.at[d + 1, k], ms_recv.at[1 - d if d else 1, col_of[k]], d, k,
                ).wait_recv()

    def gather_band(b, carry):
        for g, (main, rim, q) in enumerate(
            (
                (8, 0, 2), (16, 0, 3),
                (24, 40, 0), (32, 40, 1), (48, 40, 2), (56, 40, 3),
                (64, 80, 0), (72, 80, 1),
            )
        ):
            rows = pl.ds(pl.multiple_of(64 * b, 64) + 8 * g, 8)
            edge = mbuf[b, rim : rim + 8]
            if q:
                edge = pltpu.roll(edge, 128 - 32 * q, 1)
            xsplit[rows, 0:128] = mbuf[b, main : main + 8]
            xsplit[rows, 128:256] = edge
        return carry

    lax.fori_loop(0, BANDS, gather_band, 0)
    high, low = parts_of(xsplit[...])
    ybuf[...] = jnp.dot(
        jnp.concatenate([high, low, high], 1), ms_cols[...], preferred_element_type=jnp.float32
    )

    def finish_band(b, carry):
        g1, g2, g3 = gains[0, b], gains[1, b], gains[2, b]
        high, low = parts_of(ybuf[pl.ds(pl.multiple_of(64 * b, 64), 64)])
        total = jnp.dot(
            ms_rows[...], jnp.concatenate([high, low, high], 0), preferred_element_type=jnp.float32
        )
        total += g1 * pan_ext[PAN_RIM : PAN_RIM + ROWS]
        total += (g2 - g1) * qbuf[0] + (g3 - g2) * qbuf[1] - g3 * qbuf[2]
        out_ref[b] = total
        return carry

    lax.fori_loop(0, BANDS, finish_band, 0)

    for copy in pan_copies + ms_copies:
        copy.wait_send()


def in_hbm(x):
    return pltpu.with_memory_space_constraint(x, pltpu.HBM)


def on_device(nr, nc, tables, ms, pan, gains):
    f32 = jnp.float32
    bf16 = jnp.bfloat16
    hbm = pl.BlockSpec(memory_space=pl.ANY)
    return pl.pallas_call(
        functools.partial(kernel, nr, nc),
        out_shape=jax.ShapeDtypeStruct((BANDS, ROWS, COLS), f32),
        in_specs=[hbm] * 7,
        out_specs=pl.BlockSpec(memory_space=pltpu.VMEM),
        scratch_shapes=[
            pltpu.VMEM((LROWS, nc * LCOLS), f32),
            pltpu.VMEM((nc, 40, 128), f32),
            pltpu.VMEM((BANDS, 88, 128), f32),
            pltpu.VMEM((PAN_EXT, COLS), f32),
            pltpu.VMEM((2, 112, 128), f32),
            pltpu.VMEM((2, 112, 128), f32),
            *[pltpu.VMEM(table.shape, bf16) for table in tables],
            pltpu.VMEM((2, PAN_EXT, COLS + 128), f32),
            pltpu.VMEM((3, 3 * PAN_EXT, COLS), bf16),
            pltpu.VMEM((3, ROWS, COLS), f32),
            pltpu.VMEM((BANDS * 64, 256), f32),
            pltpu.VMEM((BANDS * 64, COLS), f32),
            pltpu.SMEM((3, BANDS), f32),
            pltpu.SemaphoreType.DMA((7,)),
            pltpu.SemaphoreType.DMA,
            pltpu.SemaphoreType.DMA((3, nc)),
            pltpu.SemaphoreType.DMA((3, nc)),
            pltpu.SemaphoreType.DMA((8,)),
            pltpu.SemaphoreType.DMA((8,)),
        ],
        compiler_params=pltpu.CompilerParams(
            collective_id=0, has_side_effects=True, vmem_limit_bytes=32 * 1024 * 1024
        ),
    )(in_hbm(ms), in_hbm(pan), in_hbm(gains.T), *[in_hbm(jnp.asarray(table)) for table in tables])


def solution(mesh):
    tables = make_tables()
    nr, nc = mesh.shape["row"], mesh.shape["col"]
    return jax.shard_map(
        functools.partial(on_device, nr, nc, tables),
        mesh=mesh,
        in_specs=(P("col", "row", None), P("row", "col"), P()),
        out_specs=P(None, "row", "col"),
        check_vma=False,
    )
```

```python
import functools
import math

import jax
import jax.numpy as jnp
import ml_dtypes
import numpy as np
from jax import lax
from jax.experimental import pallas as pl
from jax.experimental.pallas import tpu as pltpu
from jax.sharding import PartitionSpec as P

MESH = pl.DeviceIdType.MESH
BF16 = ml_dtypes.bfloat16

TAPS = [
    0.2303778133088964,
    0.7148465705529154,
    0.6308807679298587,
    -0.0279837694168599,
    -0.1870348117190931,
    0.0308413818355607,
    0.0328830116668852,
    -0.0105974017850690,
]

ROWS, COLS = 128, 512
LROWS, LCOLS = 32, 128
PAN_RIM = 48
PAN_EXT = ROWS + 2 * PAN_RIM
MS_RIM = 16
BANDS = 8


def projection(level):
    step = 2**level
    rows = [{} for _ in range(8)]
    for tree in range(2):
        taps = TAPS if tree == 0 else TAPS[::-1]
        cascade, shift = [1.0], 0
        for lev in range(level):
            longer = [0.0] * (len(cascade) + 7 * 2**lev)
            for i, value in enumerate(cascade):
                for j, tap in enumerate(taps):
                    longer[i + j * 2**lev] += value * tap
            cascade, shift = longer, shift + (3 + tree) * 2**lev
        span = len(cascade)
        for m in range(8):
            for k in range(-64, 64):
                at = m - step * k + shift
                if 0 <= at < span:
                    for i, value in enumerate(cascade):
                        offset = step * k - shift + i - m
                        rows[m][offset] = rows[m].get(offset, 0.0) + 0.5 * cascade[at] * value
    return rows


def cubic_weight(distance):
    magnitude = abs(distance)
    if magnitude <= 1.0:
        return 1.5 * magnitude**3 - 2.5 * magnitude**2 + 1.0
    if magnitude < 2.0:
        return -0.5 * magnitude**3 + 2.5 * magnitude**2 - 4.0 * magnitude + 2.0
    return 0.0


def upsampled_projection():
    rows = [{} for _ in range(8)]
    for m, weights in enumerate(projection(3)):
        for offset in sorted(weights):
            position = (m + offset + 0.5) / 4.0 - 0.5
            floor = math.floor(position)
            for low in range(floor - 1, floor + 3):
                term = weights[offset] * cubic_weight(position - low)
                rows[m][low] = rows[m].get(low, 0.0) + term
    return rows


def split_parts(matrix):
    high = matrix.astype(np.float32).astype(BF16)
    low = (matrix - high.astype(np.float64)).astype(np.float32).astype(BF16)
    return high, low


def pan_matrix(level, outs, ins, start):
    matrix = np.zeros((outs, ins))
    rows = projection(level)
    for m in range(outs):
        for offset, weight in rows[m % 8].items():
            matrix[m, m + offset - start] = weight
    return matrix


def ms_matrix(outs, lows):
    place = {low: at for at, low in lows}
    matrix = np.zeros((outs, max(at for at, _ in lows) + 1))
    rows = upsampled_projection()
    for m in range(outs):
        for low, weight in rows[m % 8].items():
            matrix[m, place[low + 2 * (m // 8)]] = weight
    return matrix


def make_tables():
    high, low = split_parts(ms_matrix(ROWS, [(i, i - MS_RIM) for i in range(LROWS + 2 * MS_RIM)]))
    ms_rows = np.concatenate([high, high, low], 1)
    lows = [(i, i) for i in range(LCOLS)]
    lows += [(LCOLS + i, i - MS_RIM) for i in range(MS_RIM)]
    lows += [(LCOLS + MS_RIM + i, LCOLS + i) for i in range(MS_RIM)]
    matrix = ms_matrix(COLS, lows)
    matrix = np.pad(matrix, ((0, 0), (0, 256 - matrix.shape[1]))).T
    high, low = split_parts(matrix)
    ms_cols = np.concatenate([high, high, low], 0)
    matrix = np.concatenate([pan_matrix(level, 128, 256, -64) for level in (1, 2, 3)], 0).T
    high, low = split_parts(matrix)
    pan_cols = np.concatenate([high, high, low], 0)
    pan_rows = []
    for level in (1, 2, 3):
        high, low = split_parts(pan_matrix(level, ROWS, PAN_EXT, -PAN_RIM))
        pan_rows.append(np.concatenate([high, high, low], 1))
    return ms_rows, ms_cols, pan_cols, np.stack(pan_rows)


def parts_of(x):
    high = x.astype(jnp.bfloat16)
    low = (x - high.astype(jnp.float32)).astype(jnp.bfloat16)
    return high, low


def spread(
    nr, nc,
    ms_hbm, pan_hbm, gains_hbm, ms_rows_hbm, ms_cols_hbm, pan_cols_hbm, pan_rows_hbm,
    terms, ysplit, ms_rows,
    ms_own, stage, mbuf, pan_ext, pstage, precv,
    ms_cols, pan_cols, pan_rows,
    pan_roll, pan_split, zbuf, qbuf, xbuf,
    gains, load_sems, own_sem, ms_send, ms_recv, pan_send, pan_recv,
):
    r, c = lax.axis_index("row"), lax.axis_index("col")
    half = nc // 2
    row_of = {d: lax.rem(r + d + nr, nr) for d in (-1, 0, 1)}
    side, place = c // half, lax.rem(c, half)
    halves = [lax.rem(side + a, 2) * half for a in range(2)]
    col_of = {
        (a, k): halves[a] + lax.rem(place + k, half) for a in range(2) for k in range(half)
    }

    ms_load = pltpu.make_async_copy(ms_hbm.at[0], ms_own, load_sems.at[0])
    pan_load = pltpu.make_async_copy(
        pan_hbm, pan_ext.at[PAN_RIM : PAN_RIM + ROWS], load_sems.at[1]
    )
    ms_load.start()
    pan_load.start()

    barrier = pltpu.get_barrier_semaphore()
    for d in (-1, 0, 1):
        for at, col in col_of.items():
            if d or at != (0, 0):
                pl.semaphore_signal(
                    barrier, inc=1, device_id=(row_of[d], col), device_id_type=MESH
                )

    table_loads = [
        pltpu.make_async_copy(source, target, load_sems.at[2 + i])
        for i, (source, target) in enumerate(
            (
                (pan_cols_hbm, pan_cols),
                (pan_rows_hbm, pan_rows),
                (gains_hbm, gains),
                (ms_cols_hbm, ms_cols),
                (ms_rows_hbm, ms_rows),
            )
        )
    ]
    for load in table_loads:
        load.start()

    lane = lax.broadcasted_iota(jnp.int32, (8, 128), 1)

    ms_load.wait()
    for dest in range(nc):
        tile = slice(128 * dest, 128 * dest + 128)
        before = (dest - 1) % nc
        after = (dest + 1) % nc
        stage[dest, 0:16] = ms_own[0:16, tile]
        stage[dest, 24:40] = ms_own[16:32, tile]
        rim = None
        for q in range(4):
            rows = slice(8 * q, 8 * q + 8)
            both = jnp.where(
                lane < 64,
                ms_own[rows, 128 * after : 128 * after + 128],
                ms_own[rows, 128 * before : 128 * before + 128],
            )
            both = pltpu.roll(both, (16 + 32 * q) % 128, 1)
            rim = both if rim is None else jnp.where(lane < 32 * q, rim, both)
        stage[dest, 16:24] = rim

    pan_load.wait()
    for at, (first, count) in ((0, (0, 64)), (64, (80, 24)), (88, (0, 24))):
        for step in range(0, count, 8):
            upper = PAN_RIM + first + step
            lower = upper + count
            for way, column in ((0, 384), (1, 0)):
                one = pan_ext[upper : upper + 8, column : column + 128]
                two = pan_ext[lower : lower + 8, column : column + 128]
                if way == 0:
                    packed = jnp.where(lane < 64, pltpu.roll(one, 64, 1), two)
                else:
                    packed = jnp.where(lane < 64, one, pltpu.roll(two, 64, 1))
                pstage[way, at + step : at + step + 8] = packed

    pl.semaphore_wait(barrier, 3 * nc - 1)

    def remote(source, target, send_sem, recv_sem, d, col):
        return pltpu.make_async_remote_copy(
            src_ref=source,
            dst_ref=target,
            send_sem=send_sem,
            recv_sem=recv_sem,
            device_id=(row_of[d], col),
            device_id_type=MESH,
        )

    pan_copies = []
    own = PAN_RIM
    for d, source, target in (
        (1, pan_ext.at[own + ROWS - PAN_RIM : own + ROWS], pan_ext.at[0:PAN_RIM]),
        (-1, pan_ext.at[own : own + PAN_RIM], pan_ext.at[own + ROWS : PAN_EXT]),
    ):
        at = len(pan_copies)
        pan_copies.append(remote(source, target, pan_send.at[at], pan_recv.at[at], d, c))
    for way, k in ((0, 1), (1, nc - 1)):
        for d, rows in ((0, slice(0, 64)), (1, slice(64, 88)), (-1, slice(88, 112))):
            at = len(pan_copies)
            pan_copies.append(
                remote(
                    pstage.at[way, rows], precv.at[way, rows],
                    pan_send.at[at], pan_recv.at[at], d, lax.rem(c + k, nc),
                )
            )
    spans = {
        0: (slice(0, 40), slice(24, 64)),
        1: (slice(16, 40), slice(0, 24)),
        -1: (slice(0, 24), slice(64, 88)),
    }
    ms_copies = []
    for a in (1, 0):
        for k in range(half):
            for d in (0, 1, -1):
                if a or k or d:
                    source, target = spans[d]
                    ms_copies.append(
                        remote(
                            stage.at[col_of[a, k], source], mbuf.at[c, target],
                            ms_send.at[d + 1, half * a + k], ms_recv.at[d + 1, c],
                            d, col_of[a, k],
                        )
                    )
    own_copy = pltpu.make_async_copy(stage.at[c], mbuf.at[c, 24:64], own_sem)
    for copy in pan_copies + ms_copies:
        copy.start()
    own_copy.start()

    for copy in pan_copies:
        copy.wait_recv()
    for step in range(0, PAN_EXT, 8):
        rows = slice(step, step + 8)
        if step < 48:
            base, at, count = 0, 64, 24
        elif step < 176:
            base, at, count = 48, 0, 64
        else:
            base, at, count = 176, 88, 24
        second = step - base >= count
        inside = step - base - (count if second else 0)
        left = precv[0, at + inside : at + inside + 8]
        right = precv[1, at + inside : at + inside + 8]
        if second:
            left = pltpu.roll(left, 64, 1)
        else:
            right = pltpu.roll(right, 64, 1)
        tiles = [left]
        tiles += [pltpu.roll(pan_ext[rows, 128 * t : 128 * t + 128], 64, 1) for t in range(4)]
        tiles += [right]
        for t in range(5):
            pan_roll[rows, 128 * t : 128 * t + 128] = jnp.where(lane < 64, tiles[t], tiles[t + 1])
    pan_split[0], pan_split[1] = parts_of(pan_roll[...])

    for load in table_loads:
        load.wait()
    for j in range(4):
        window = slice(128 * j, 128 * j + 256)
        high, low = pan_split[0, :, window], pan_split[1, :, window]
        z = jnp.dot(
            jnp.concatenate([high, low, high], 1), pan_cols[...], preferred_element_type=jnp.float32
        )
        for level in range(3):
            high, low = parts_of(z[:, 128 * level : 128 * level + 128])
            for at, part in ((0, high), (1, low), (2, high)):
                zbuf[level, PAN_EXT * at : PAN_EXT * (at + 1), 128 * j : 128 * j + 128] = part
    for level in range(3):
        qbuf[level] = jnp.dot(pan_rows[level], zbuf[level], preferred_element_type=jnp.float32)

    def weigh(step, carry):
        rows = pl.ds(pl.multiple_of(8 * step, 8), 8)
        own_rows = pl.ds(pl.multiple_of(8 * step + PAN_RIM, 8), 8)
        fields = [pan_ext[own_rows, :]] + [qbuf[level, rows, :] for level in range(3)]
        for b in range(BANDS):
            g1, g2, g3 = gains[0, b], gains[1, b], gains[2, b]
            terms[b, rows, :] = (
                g1 * fields[0] + (g2 - g1) * fields[1] + (g3 - g2) * fields[2] - g3 * fields[3]
            )
        return carry

    lax.fori_loop(0, ROWS // 8, weigh, 0)

    own_copy.wait()
    for a in range(2):
        for k in range(half):
            for d in (-1, 0, 1):
                if a or k or d:
                    source, target = spans[d]
                    sender = col_of[a, k]
                    remote(
                        stage.at[sender, source], mbuf.at[sender, target],
                        ms_send.at[d + 1, half * a + k], ms_recv.at[d + 1, sender],
                        d, sender,
                    ).wait_recv()
        for k in range(half):
            b = halves[a] + k
            for g, (main, rim, q) in enumerate(
                (
                    (8, 0, 2), (16, 0, 3),
                    (24, 40, 0), (32, 40, 1), (48, 40, 2), (56, 40, 3),
                    (64, 80, 0), (72, 80, 1),
                )
            ):
                rows = slice(64 * k + 8 * g, 64 * k + 8 * g + 8)
                edge = mbuf[b, rim : rim + 8]
                if q:
                    edge = pltpu.roll(edge, 128 - 32 * q, 1)
                xbuf[rows, 0:128] = mbuf[b, main : main + 8]
                xbuf[rows, 128:256] = edge
        high, low = parts_of(xbuf[...])
        y = jnp.dot(
            jnp.concatenate([high, low, high], 1), ms_cols[...], preferred_element_type=jnp.float32
        )
        high, low = parts_of(y)
        for k in range(half):
            ysplit[halves[a] + k, 0:64] = high[64 * k : 64 * k + 64]
            ysplit[halves[a] + k, 64:128] = low[64 * k : 64 * k + 64]

    for copy in pan_copies + ms_copies:
        copy.wait_send()


def finish(terms, ysplit, ms_rows, out_hbm, result, sems):
    copies = []
    for b in range(BANDS):
        high = ysplit[b, 0:64]
        column = jnp.concatenate([high, ysplit[b, 64:128], high], 0)
        result[b] = terms[b] + jnp.dot(ms_rows[...], column, preferred_element_type=jnp.float32)
        copies.append(pltpu.make_async_copy(result.at[b], out_hbm.at[b], sems.at[b]))
        copies[-1].start()
    for copy in copies:
        copy.wait()


def in_hbm(x):
    return pltpu.with_memory_space_constraint(x, pltpu.HBM)


def on_device(nr, nc, tables, ms, pan, gains):
    f32 = jnp.float32
    bf16 = jnp.bfloat16
    hbm = pl.BlockSpec(memory_space=pl.ANY)
    vmem = pl.BlockSpec(memory_space=pltpu.VMEM)
    shared = pl.pallas_call(
        functools.partial(spread, nr, nc),
        out_shape=[
            pltpu.VMEM((BANDS, ROWS, COLS), f32),
            pltpu.VMEM((BANDS, 128, COLS), bf16),
            pltpu.VMEM(tables[0].shape, bf16),
        ],
        in_specs=[hbm] * 7,
        out_specs=[vmem] * 3,
        scratch_shapes=[
            pltpu.VMEM((LROWS, nc * LCOLS), f32),
            pltpu.VMEM((nc, 40, 128), f32),
            pltpu.VMEM((BANDS, 88, 128), f32),
            pltpu.VMEM((PAN_EXT, COLS), f32),
            pltpu.VMEM((2, 112, 128), f32),
            pltpu.VMEM((2, 112, 128), f32),
            *[pltpu.VMEM(table.shape, bf16) for table in tables[1:]],
            pltpu.VMEM((PAN_EXT, COLS + 128), f32),
            pltpu.VMEM((2, PAN_EXT, COLS + 128), bf16),
            pltpu.VMEM((3, 3 * PAN_EXT, COLS), bf16),
            pltpu.VMEM((3, ROWS, COLS), f32),
            pltpu.VMEM((BANDS * 32, 256), f32),
            pltpu.SMEM((3, BANDS), f32),
            pltpu.SemaphoreType.DMA((7,)),
            pltpu.SemaphoreType.DMA,
            pltpu.SemaphoreType.DMA((3, nc)),
            pltpu.SemaphoreType.DMA((3, nc)),
            pltpu.SemaphoreType.DMA((8,)),
            pltpu.SemaphoreType.DMA((8,)),
        ],
        compiler_params=pltpu.CompilerParams(
            collective_id=0, has_side_effects=True, vmem_limit_bytes=32 * 1024 * 1024
        ),
    )(in_hbm(ms), in_hbm(pan), in_hbm(gains.T), *[in_hbm(jnp.asarray(table)) for table in tables])
    return pl.pallas_call(
        finish,
        out_shape=jax.ShapeDtypeStruct((BANDS, ROWS, COLS), f32),
        in_specs=[vmem] * 3,
        out_specs=hbm,
        scratch_shapes=[pltpu.VMEM((BANDS, ROWS, COLS), f32), pltpu.SemaphoreType.DMA((BANDS,))],
        compiler_params=pltpu.CompilerParams(vmem_limit_bytes=16 * 1024 * 1024),
    )(*shared)


def solution(mesh):
    tables = make_tables()
    nr, nc = mesh.shape["row"], mesh.shape["col"]
    return jax.shard_map(
        functools.partial(on_device, nr, nc, tables),
        mesh=mesh,
        in_specs=(P("col", "row", None), P("row", "col"), P()),
        out_specs=P(None, "row", "col"),
        check_vma=False,
    )
```

```python
import functools
import math

import jax
import jax.numpy as jnp
import ml_dtypes
import numpy as np
from jax import lax
from jax.experimental import pallas as pl
from jax.experimental.pallas import tpu as pltpu
from jax.sharding import PartitionSpec as P

MESH = pl.DeviceIdType.MESH
BF16 = ml_dtypes.bfloat16

TAPS = [
    0.2303778133088964,
    0.7148465705529154,
    0.6308807679298587,
    -0.0279837694168599,
    -0.1870348117190931,
    0.0308413818355607,
    0.0328830116668852,
    -0.0105974017850690,
]

ROWS, COLS = 128, 512
LROWS, LCOLS = 32, 128
PAN_RIM = 32
PAN_SENT = 48
PAN_EXT = ROWS + 2 * PAN_RIM
MS_RIM = 16
BANDS = 8

RIM_PIECES = [(3 * j, 3, (0, 26 * j), 3, 29) for j in range(4)]
RIM_PIECES += [(12, 1, (0, 104), 3, 16), (12, 1, (1, 104), 16, 29)]


def windows(level):
    found = []
    for tree in range(2):
        taps = TAPS if tree == 0 else TAPS[::-1]
        cascade, shift = [1.0], 0
        for lev in range(level):
            longer = [0.0] * (len(cascade) + 7 * 2**lev)
            for i, value in enumerate(cascade):
                for j, tap in enumerate(taps):
                    longer[i + j * 2**lev] += value * tap
            cascade, shift = longer, shift + (3 + tree) * 2**lev
        found.append((2**level, shift, cascade))
    return found


def projection(level):
    rows = [{} for _ in range(8)]
    for step, shift, cascade in windows(level):
        for m in range(8):
            for k in range(-64, 64):
                at = m - step * k + shift
                if 0 <= at < len(cascade):
                    for i, value in enumerate(cascade):
                        offset = step * k - shift + i - m
                        rows[m][offset] = rows[m].get(offset, 0.0) + 0.5 * cascade[at] * value
    return rows


def cubic_weight(distance):
    magnitude = abs(distance)
    if magnitude <= 1.0:
        return 1.5 * magnitude**3 - 2.5 * magnitude**2 + 1.0
    if magnitude < 2.0:
        return -0.5 * magnitude**3 + 2.5 * magnitude**2 - 4.0 * magnitude + 2.0
    return 0.0


def upsampled_projection():
    rows = [{} for _ in range(8)]
    for m, weights in enumerate(projection(3)):
        for offset in sorted(weights):
            position = (m + offset + 0.5) / 4.0 - 0.5
            floor = math.floor(position)
            for low in range(floor - 1, floor + 3):
                term = weights[offset] * cubic_weight(position - low)
                rows[m][low] = rows[m].get(low, 0.0) + term
    return rows


def split_parts(matrix):
    high = matrix.astype(np.float32).astype(BF16)
    low = (matrix - high.astype(np.float64)).astype(np.float32).astype(BF16)
    return high, low


def pan_matrix(level, outs, ins, start):
    matrix = np.zeros((outs, ins))
    rows = projection(level)
    for m in range(outs):
        for offset, weight in rows[m % 8].items():
            if 0 <= m + offset - start < ins:
                matrix[m, m + offset - start] = weight
    return matrix


def straddling(edge):
    found = []
    for level in (1, 2, 3):
        for step, shift, cascade in windows(level):
            for k in range(-64, 128):
                first = step * k - shift
                if first < edge < first + len(cascade):
                    found.append((level, first, cascade))
    return found


def row_tables():
    above, below = straddling(0), straddling(ROWS)
    down = np.zeros((PAN_RIM, PAN_SENT))
    up = np.zeros((PAN_RIM, PAN_SENT))
    merged = np.zeros((3, ROWS, PAN_EXT))
    for level in (1, 2, 3):
        merged[level - 1, :, PAN_RIM : PAN_RIM + ROWS] = pan_matrix(level, ROWS, ROWS, 0)
    for at, (level, first, cascade) in enumerate(above):
        for i, weight in enumerate(cascade):
            if first + i < 0:
                down[at, first + i + PAN_SENT] = weight
            else:
                merged[level - 1, first + i, at] = 0.5 * weight
    for at, (level, first, cascade) in enumerate(below):
        for i, weight in enumerate(cascade):
            if first + i >= ROWS:
                up[at, first + i - ROWS] = weight
            else:
                merged[level - 1, first + i, PAN_RIM + ROWS + at] = 0.5 * weight
    return down, up, merged


def ms_matrix(outs, ins, lows):
    place = {low: at for at, low in lows}
    matrix = np.zeros((outs, ins))
    rows = upsampled_projection()
    for m in range(outs):
        for low, weight in rows[m % 8].items():
            matrix[m, place[low + 2 * (m // 8)]] = weight
    return matrix


def make_tables():
    ms_rows = []
    for odd in (0, 1):
        inner, outer = (-16, 32) if odd else (32, -13)
        lows = [(i, i) for i in range(LROWS)]
        lows += [(LROWS + i, inner + i) for i in range(16)]
        lows += [(LROWS + 19 + i, outer + i) for i in range(13)]
        high, low = split_parts(ms_matrix(ROWS, 64, lows))
        ms_rows.append(np.concatenate([high, high, low], 1))
    lows = [(i, i) for i in range(LCOLS)]
    lows += [(LCOLS + i, i - MS_RIM) for i in range(MS_RIM)]
    lows += [(LCOLS + MS_RIM + i, LCOLS + i) for i in range(MS_RIM)]
    high, low = split_parts(ms_matrix(COLS, 256, lows).T)
    ms_cols = np.concatenate([high, high, low], 0)
    matrix = np.concatenate([pan_matrix(level, 128, 256, -64) for level in (1, 2, 3)], 0).T
    high, low = split_parts(matrix)
    pan_cols = np.concatenate([high, high, low], 0)
    sums, pan_rows = [], []
    down, up, merged = row_tables()
    for matrix in (down, up):
        high, low = split_parts(matrix)
        sums.append(np.concatenate([high, high, low], 1))
    for level in range(3):
        high, low = split_parts(merged[level])
        pan_rows.append(np.concatenate([high, high, low], 1))
    return np.stack(ms_rows), ms_cols, pan_cols, np.stack(pan_rows), np.stack(sums)


def parts_of(x):
    high = x.astype(jnp.bfloat16)
    low = (x - high.astype(jnp.float32)).astype(jnp.bfloat16)
    return high, low


def spread(
    nr, nc,
    ms_hbm, pan_hbm, gains_hbm, ms_rows_hbm, ms_cols_hbm, pan_cols_hbm, pan_rows_hbm, sums_hbm,
    terms, ysplit, ms_rows,
    ms_own, stage, ostage, mbuf, obuf, pan_ext, psums, pstage, precv,
    ms_cols, pan_cols, pan_rows, sums,
    pan_roll, pan_split, zbuf, qbuf, xbuf,
    gains, load_sems, own_sem, ms_send, ms_recv, pan_send, pan_recv,
):
    r, c = lax.axis_index("row"), lax.axis_index("col")
    half = nc // 2
    row_of = {d: lax.rem(r + d + nr, nr) for d in (-1, 0, 1)}
    side, place = c // half, lax.rem(c, half)
    halves = [lax.rem(side + a, 2) * half for a in range(2)]
    col_of = {
        (a, k): halves[a] + lax.rem(place + k, half) for a in range(2) for k in range(half)
    }

    ms_load = pltpu.make_async_copy(ms_hbm.at[0], ms_own, load_sems.at[0])
    pan_load = pltpu.make_async_copy(
        pan_hbm, pan_ext.at[PAN_RIM : PAN_RIM + ROWS], load_sems.at[1]
    )
    sums_load = pltpu.make_async_copy(sums_hbm, sums, load_sems.at[7])
    ms_load.start()
    pan_load.start()
    sums_load.start()

    odd = lax.rem(r, 2)
    inner = lax.rem(r + 1 - 2 * odd + nr, nr)
    outer = lax.rem(r - 1 + 2 * odd + nr, nr)

    barrier = pltpu.get_barrier_semaphore()
    for col in col_of.values():
        pl.semaphore_signal(barrier, inc=1, device_id=(outer, col), device_id_type=MESH)
    for at, col in col_of.items():
        if at != (0, 0):
            pl.semaphore_signal(barrier, inc=1, device_id=(r, col), device_id_type=MESH)
    for k in (0, 1, nc - 1):
        pl.semaphore_signal(
            barrier, inc=1, device_id=(inner, lax.rem(c + k, nc)), device_id_type=MESH
        )

    table_loads = [
        pltpu.make_async_copy(source, target, load_sems.at[2 + i])
        for i, (source, target) in enumerate(
            (
                (pan_cols_hbm, pan_cols),
                (pan_rows_hbm, pan_rows),
                (gains_hbm, gains),
                (ms_cols_hbm, ms_cols),
                (ms_rows_hbm.at[odd], ms_rows),
            )
        )
    ]
    for load in table_loads:
        load.start()

    lane = lax.broadcasted_iota(jnp.int32, (8, 128), 1)
    sublane = lax.broadcasted_iota(jnp.int32, (8, 128), 0)

    ms_load.wait()
    for dest in range(nc):
        tile = slice(128 * dest, 128 * dest + 128)
        before = (dest - 1) % nc
        after = (dest + 1) % nc
        stage[dest, 0:16] = ms_own[0:16, tile]
        stage[dest, 24:40] = ms_own[16:32, tile]
        rim = None
        for q in range(4):
            rows = slice(8 * q, 8 * q + 8)
            both = jnp.where(
                lane < 64,
                ms_own[rows, 128 * after : 128 * after + 128],
                ms_own[rows, 128 * before : 128 * before + 128],
            )
            both = pltpu.roll(both, (16 + 32 * q) % 128, 1)
            rim = both if rim is None else jnp.where(lane < 32 * q, rim, both)
        stage[dest, 16:24] = rim

    for way in range(2):

        @pl.when(odd == way)
        def _():
            for dest in range(nc):
                tile = slice(128 * dest, 128 * dest + 128)
                if way:
                    upper, lower = ms_own[16:24, tile], ms_own[24:32, tile]
                else:
                    upper = pltpu.roll(ms_own[0:8, tile], 3, 0)
                    lower = jnp.where(sublane < 3, upper, pltpu.roll(ms_own[8:16, tile], 3, 0))
                rim = stage[dest, 16:24]
                for i, count, at, first, last in RIM_PIECES:
                    row = i + 19 * way
                    while count:
                        q, sub = row // 8, row % 8
                        now = min(count, 8 - sub)
                        moved = pltpu.roll(rim, (at[0] - sub) % 8, 0)
                        moved = pltpu.roll(moved, (at[1] - 32 * q - first) % 128, 1)
                        inside = (sublane >= at[0]) & (sublane < at[0] + now)
                        inside &= (lane >= at[1]) & (lane < at[1] + last - first)
                        upper = jnp.where(inside, moved, upper)
                        row, count, at = row + now, count - now, (at[0] + now, at[1])
                ostage[dest, 0:8] = upper
                ostage[dest, 8:16] = lower

    pan_load.wait()
    sums_load.wait()
    for way, first in ((0, PAN_RIM + ROWS - PAN_SENT), (1, PAN_RIM)):
        high, low = parts_of(pan_ext[first : first + PAN_SENT])
        psums[way] = jnp.dot(
            sums[way], jnp.concatenate([high, low, high], 0), preferred_element_type=jnp.float32
        )
    for at, source, first, count in (
        (0, pan_ext, PAN_RIM, 64), (64, psums.at[0], 0, 16), (80, psums.at[1], 0, 16)
    ):
        for step in range(0, count, 8):
            upper = first + step
            lower = upper + count
            for way, column in ((0, 384), (1, 0)):
                one = source[upper : upper + 8, column : column + 128]
                two = source[lower : lower + 8, column : column + 128]
                if way == 0:
                    packed = jnp.where(lane < 64, pltpu.roll(one, 64, 1), two)
                else:
                    packed = jnp.where(lane < 64, one, pltpu.roll(two, 64, 1))
                pstage[way, at + step : at + step + 8] = packed

    pl.semaphore_wait(barrier, 2 * nc + 2)

    def remote(source, target, send_sem, recv_sem, row, col):
        return pltpu.make_async_remote_copy(
            src_ref=source,
            dst_ref=target,
            send_sem=send_sem,
            recv_sem=recv_sem,
            device_id=(row, col),
            device_id_type=MESH,
        )

    pan_copies = []
    for d, source, target in (
        (1, psums.at[0], pan_ext.at[0:PAN_RIM]),
        (-1, psums.at[1], pan_ext.at[PAN_RIM + ROWS : PAN_EXT]),
    ):
        at = len(pan_copies)
        pan_copies.append(remote(source, target, pan_send.at[at], pan_recv.at[at], row_of[d], c))
    for way, k in ((0, 1), (1, nc - 1)):
        for d, rows in ((0, slice(0, 64)), (1, slice(64, 80)), (-1, slice(80, 96))):
            at = len(pan_copies)
            pan_copies.append(
                remote(
                    pstage.at[way, rows], precv.at[way, rows],
                    pan_send.at[at], pan_recv.at[at], row_of[d], lax.rem(c + k, nc),
                )
            )
    def rows_of(first, count):
        return pl.ds(pl.multiple_of(first, 8), count)

    same_copies, outer_copies = [], []
    for a in (1, 0):
        for k in range(half):
            col = col_of[a, k]
            at = half * a + k
            if a or k:
                same_copies.append(
                    remote(
                        stage.at[col], mbuf.at[c, 0:40],
                        ms_send.at[0, at], ms_recv.at[0, c], r, col,
                    )
                )
            outer_copies.append(
                remote(
                    ostage.at[col], obuf.at[c],
                    ms_send.at[1, at], ms_recv.at[1, c], outer, col,
                )
            )
    own_copy = pltpu.make_async_copy(stage.at[c], mbuf.at[c, 0:40], own_sem)
    own_copy.start()
    for copy in same_copies + pan_copies + outer_copies:
        copy.start()

    own_copy.wait()
    inner_copies = []
    for a in (0, 1):
        for k in range(half):
            if a or k:
                sender = col_of[a, k]
                remote(
                    stage.at[sender], mbuf.at[sender, 0:40],
                    ms_send.at[0, half * a + k], ms_recv.at[0, sender], r, sender,
                ).wait_recv()
        bands = pl.ds(halves[a], half)
        inner_copies.append(
            remote(
                mbuf.at[bands, rows_of(16 - 16 * odd, 24)], mbuf.at[bands, 40:64],
                ms_send.at[2, a], ms_recv.at[2, a], inner, c,
            )
        )
        inner_copies[-1].start()

    for copy in pan_copies:
        copy.wait_recv()
    for step in range(0, PAN_EXT, 8):
        rows = slice(step, step + 8)
        if step < PAN_RIM:
            base, at, count = 0, 64, 16
        elif step < PAN_RIM + ROWS:
            base, at, count = PAN_RIM, 0, 64
        else:
            base, at, count = PAN_RIM + ROWS, 80, 16
        second = step - base >= count
        inside = step - base - (count if second else 0)
        left = precv[0, at + inside : at + inside + 8]
        right = precv[1, at + inside : at + inside + 8]
        if second:
            left = pltpu.roll(left, 64, 1)
        else:
            right = pltpu.roll(right, 64, 1)
        tiles = [left]
        tiles += [pltpu.roll(pan_ext[rows, 128 * t : 128 * t + 128], 64, 1) for t in range(4)]
        tiles += [right]
        for t in range(5):
            pan_roll[rows, 128 * t : 128 * t + 128] = jnp.where(lane < 64, tiles[t], tiles[t + 1])
    pan_split[0], pan_split[1] = parts_of(pan_roll[...])

    for load in table_loads:
        load.wait()
    for j in range(4):
        window = slice(128 * j, 128 * j + 256)
        high, low = pan_split[0, :, window], pan_split[1, :, window]
        z = jnp.dot(
            jnp.concatenate([high, low, high], 1), pan_cols[...], preferred_element_type=jnp.float32
        )
        for level in range(3):
            high, low = parts_of(z[:, 128 * level : 128 * level + 128])
            for at, part in ((0, high), (1, low), (2, high)):
                zbuf[level, PAN_EXT * at : PAN_EXT * (at + 1), 128 * j : 128 * j + 128] = part
    for level in range(3):
        qbuf[level] = jnp.dot(pan_rows[level], zbuf[level], preferred_element_type=jnp.float32)

    def weigh(step, carry):
        rows = pl.ds(pl.multiple_of(8 * step, 8), 8)
        own_rows = pl.ds(pl.multiple_of(8 * step + PAN_RIM, 8), 8)
        fields = [pan_ext[own_rows, :]] + [qbuf[level, rows, :] for level in range(3)]
        for b in range(BANDS):
            g1, g2, g3 = gains[0, b], gains[1, b], gains[2, b]
            terms[b, rows, :] = (
                g1 * fields[0] + (g2 - g1) * fields[1] + (g3 - g2) * fields[2] - g3 * fields[3]
            )
        return carry

    lax.fori_loop(0, ROWS // 8, weigh, 0)

    for a in range(2):
        inner_copies[a].wait_recv()
        for k in range(half):
            sender = col_of[a, k]
            remote(
                ostage.at[sender], obuf.at[sender],
                ms_send.at[1, half * a + k], ms_recv.at[1, sender], outer, sender,
            ).wait_recv()
        for k in range(half):
            b = halves[a] + k
            parts = [(mbuf[b, m : m + 8], mbuf[b, 16:24], 32 * q) for q, m in enumerate((0, 8, 24, 32))]
            rim = mbuf[b, rows_of(56 - 16 * odd, 8)]
            for q in range(2):
                parts.append((mbuf[b, rows_of(40 + 8 * odd + 8 * q, 8)], rim, 32 * q + 64 * odd))
            for g, (main, rim, at) in enumerate(parts):
                rows = slice(64 * k + 8 * g, 64 * k + 8 * g + 8)
                xbuf[rows, 0:128] = main
                xbuf[rows, 128:256] = pltpu.roll(rim, lax.rem(128 - at, 128), 1)
            upper, lower = obuf[b, 0:8], obuf[b, 8:16]
            rims = [upper, lower]
            for i, count, at, first, last in RIM_PIECES:
                moved = pltpu.roll(upper, (i + 3 - at[0]) % 8, 0)
                moved = pltpu.roll(moved, (first - at[1]) % 128, 1)
                for v in range(2):
                    low, high = i + 3 - 8 * v, i + 3 + count - 8 * v
                    if low < 8 and high > 0:
                        inside = (sublane >= low) & (sublane < high)
                        if last - first < 26:
                            inside &= (lane >= first) & (lane < last)
                        rims[v] = jnp.where(inside, moved, rims[v])
            for v, main in enumerate((upper, lower)):
                rows = slice(64 * k + 48 + 8 * v, 64 * k + 56 + 8 * v)
                xbuf[rows, 0:128] = main
                xbuf[rows, 128:256] = rims[v]
        high, low = parts_of(xbuf[...])
        y = jnp.dot(
            jnp.concatenate([high, low, high], 1), ms_cols[...], preferred_element_type=jnp.float32
        )
        high, low = parts_of(y)
        for k in range(half):
            ysplit[halves[a] + k, 0:64] = high[64 * k : 64 * k + 64]
            ysplit[halves[a] + k, 64:128] = low[64 * k : 64 * k + 64]

    for copy in same_copies + pan_copies + outer_copies + inner_copies:
        copy.wait_send()


def finish(terms, ysplit, ms_rows, out_hbm, result, sems):
    copies = []
    for b in range(BANDS):
        high = ysplit[b, 0:64]
        column = jnp.concatenate([high, ysplit[b, 64:128], high], 0)
        result[b] = terms[b] + jnp.dot(ms_rows[...], column, preferred_element_type=jnp.float32)
        copies.append(pltpu.make_async_copy(result.at[b], out_hbm.at[b], sems.at[b]))
        copies[-1].start()
    for copy in copies:
        copy.wait()


def in_hbm(x):
    return pltpu.with_memory_space_constraint(x, pltpu.HBM)


def on_device(nr, nc, tables, ms, pan, gains):
    f32 = jnp.float32
    bf16 = jnp.bfloat16
    hbm = pl.BlockSpec(memory_space=pl.ANY)
    vmem = pl.BlockSpec(memory_space=pltpu.VMEM)
    shared = pl.pallas_call(
        functools.partial(spread, nr, nc),
        out_shape=[
            pltpu.VMEM((BANDS, ROWS, COLS), f32),
            pltpu.VMEM((BANDS, 128, COLS), bf16),
            pltpu.VMEM(tables[0].shape[1:], bf16),
        ],
        in_specs=[hbm] * 8,
        out_specs=[vmem] * 3,
        scratch_shapes=[
            pltpu.VMEM((LROWS, nc * LCOLS), f32),
            pltpu.VMEM((nc, 40, 128), f32),
            pltpu.VMEM((nc, 16, 128), f32),
            pltpu.VMEM((BANDS, 64, 128), f32),
            pltpu.VMEM((BANDS, 16, 128), f32),
            pltpu.VMEM((PAN_EXT, COLS), f32),
            pltpu.VMEM((2, PAN_RIM, COLS), f32),
            pltpu.VMEM((2, 96, 128), f32),
            pltpu.VMEM((2, 96, 128), f32),
            *[pltpu.VMEM(table.shape, bf16) for table in tables[1:]],
            pltpu.VMEM((PAN_EXT, COLS + 128), f32),
            pltpu.VMEM((2, PAN_EXT, COLS + 128), bf16),
            pltpu.VMEM((3, 3 * PAN_EXT, COLS), bf16),
            pltpu.VMEM((3, ROWS, COLS), f32),
            pltpu.VMEM((BANDS * 32, 256), f32),
            pltpu.SMEM((3, BANDS), f32),
            pltpu.SemaphoreType.DMA((8,)),
            pltpu.SemaphoreType.DMA,
            pltpu.SemaphoreType.DMA((3, nc)),
            pltpu.SemaphoreType.DMA((3, nc)),
            pltpu.SemaphoreType.DMA((8,)),
            pltpu.SemaphoreType.DMA((8,)),
        ],
        compiler_params=pltpu.CompilerParams(
            collective_id=0, has_side_effects=True, vmem_limit_bytes=32 * 1024 * 1024
        ),
    )(in_hbm(ms), in_hbm(pan), in_hbm(gains.T), *[in_hbm(jnp.asarray(table)) for table in tables])
    return pl.pallas_call(
        finish,
        out_shape=jax.ShapeDtypeStruct((BANDS, ROWS, COLS), f32),
        in_specs=[vmem] * 3,
        out_specs=hbm,
        scratch_shapes=[pltpu.VMEM((BANDS, ROWS, COLS), f32), pltpu.SemaphoreType.DMA((BANDS,))],
        compiler_params=pltpu.CompilerParams(vmem_limit_bytes=16 * 1024 * 1024),
    )(*shared)


def solution(mesh):
    tables = make_tables()
    nr, nc = mesh.shape["row"], mesh.shape["col"]
    return jax.shard_map(
        functools.partial(on_device, nr, nc, tables),
        mesh=mesh,
        in_specs=(P("col", "row", None), P("row", "col"), P()),
        out_specs=P(None, "row", "col"),
        check_vma=False,
    )
```

```python
import functools
import math

import jax
import jax.numpy as jnp
import ml_dtypes
import numpy as np
from jax import lax
from jax.experimental import pallas as pl
from jax.experimental.pallas import tpu as pltpu
from jax.sharding import PartitionSpec as P

MESH = pl.DeviceIdType.MESH
BF16 = ml_dtypes.bfloat16

TAPS = [
    0.2303778133088964,
    0.7148465705529154,
    0.6308807679298587,
    -0.0279837694168599,
    -0.1870348117190931,
    0.0308413818355607,
    0.0328830116668852,
    -0.0105974017850690,
]

ROWS, COLS = 128, 512
LROWS, LCOLS = 32, 128
PAN_RIM = 32
PAN_SENT = 48
PAN_EXT = ROWS + 2 * PAN_RIM
MS_RIM = 16
BANDS = 8

RIM_PIECES = [(3 * j, 3, (0, 26 * j), 3, 29) for j in range(4)]
RIM_PIECES += [(12, 1, (0, 104), 3, 16), (12, 1, (1, 104), 16, 29)]


def windows(level):
    found = []
    for tree in range(2):
        taps = TAPS if tree == 0 else TAPS[::-1]
        cascade, shift = [1.0], 0
        for lev in range(level):
            longer = [0.0] * (len(cascade) + 7 * 2**lev)
            for i, value in enumerate(cascade):
                for j, tap in enumerate(taps):
                    longer[i + j * 2**lev] += value * tap
            cascade, shift = longer, shift + (3 + tree) * 2**lev
        found.append((2**level, shift, cascade))
    return found


def projection(level):
    rows = [{} for _ in range(8)]
    for step, shift, cascade in windows(level):
        for m in range(8):
            for k in range(-64, 64):
                at = m - step * k + shift
                if 0 <= at < len(cascade):
                    for i, value in enumerate(cascade):
                        offset = step * k - shift + i - m
                        rows[m][offset] = rows[m].get(offset, 0.0) + 0.5 * cascade[at] * value
    return rows


def cubic_weight(distance):
    magnitude = abs(distance)
    if magnitude <= 1.0:
        return 1.5 * magnitude**3 - 2.5 * magnitude**2 + 1.0
    if magnitude < 2.0:
        return -0.5 * magnitude**3 + 2.5 * magnitude**2 - 4.0 * magnitude + 2.0
    return 0.0


def upsampled_projection():
    rows = [{} for _ in range(8)]
    for m, weights in enumerate(projection(3)):
        for offset in sorted(weights):
            position = (m + offset + 0.5) / 4.0 - 0.5
            floor = math.floor(position)
            for low in range(floor - 1, floor + 3):
                term = weights[offset] * cubic_weight(position - low)
                rows[m][low] = rows[m].get(low, 0.0) + term
    return rows


def split_parts(matrix):
    high = matrix.astype(np.float32).astype(BF16)
    low = (matrix - high.astype(np.float64)).astype(np.float32).astype(BF16)
    return high, low


def pan_matrix(level, outs, ins, start):
    matrix = np.zeros((outs, ins))
    rows = projection(level)
    for m in range(outs):
        for offset, weight in rows[m % 8].items():
            if 0 <= m + offset - start < ins:
                matrix[m, m + offset - start] = weight
    return matrix


def straddling(edge):
    found = []
    for level in (1, 2, 3):
        for step, shift, cascade in windows(level):
            for k in range(-64, 128):
                first = step * k - shift
                if first < edge < first + len(cascade):
                    found.append((level, first, cascade))
    return found


def row_tables():
    above, below = straddling(0), straddling(ROWS)
    down = np.zeros((PAN_RIM, PAN_SENT))
    up = np.zeros((PAN_RIM, PAN_SENT))
    merged = np.zeros((3, ROWS, PAN_EXT))
    for level in (1, 2, 3):
        merged[level - 1, :, :ROWS] = pan_matrix(level, ROWS, ROWS, 0)
    for at, (level, first, cascade) in enumerate(above):
        for i, weight in enumerate(cascade):
            if first + i < 0:
                down[at, first + i + PAN_SENT] = weight
            else:
                merged[level - 1, first + i, ROWS + at] = 0.5 * weight
    for at, (level, first, cascade) in enumerate(below):
        for i, weight in enumerate(cascade):
            if first + i >= ROWS:
                up[at, first + i - ROWS] = weight
            else:
                merged[level - 1, first + i, ROWS + PAN_RIM + at] = 0.5 * weight
    return down, up, merged


def ms_matrix(outs, ins, lows):
    place = {low: at for at, low in lows}
    matrix = np.zeros((outs, ins))
    rows = upsampled_projection()
    for m in range(outs):
        for low, weight in rows[m % 8].items():
            matrix[m, place[low + 2 * (m // 8)]] = weight
    return matrix


def make_tables():
    ms_rows = []
    for odd in (0, 1):
        inner, outer = (-16, 32) if odd else (32, -13)
        lows = [(i, i) for i in range(LROWS)]
        lows += [(LROWS + i, inner + i) for i in range(16)]
        lows += [(LROWS + 19 + i, outer + i) for i in range(13)]
        high, low = split_parts(ms_matrix(ROWS, 64, lows))
        ms_rows.append(np.concatenate([high, high, low], 1))
    lows = [(i, i) for i in range(LCOLS)]
    lows += [(LCOLS + i, i - MS_RIM) for i in range(MS_RIM)]
    lows += [(LCOLS + MS_RIM + i, LCOLS + i) for i in range(MS_RIM)]
    high, low = split_parts(ms_matrix(COLS, 256, lows).T)
    ms_cols = np.concatenate([high, high, low], 0)
    matrix = np.concatenate([pan_matrix(level, 128, 256, -64) for level in (1, 2, 3)], 0).T
    high, low = split_parts(matrix)
    pan_cols = np.concatenate([high, high, low], 0)
    sums, pan_rows = [], []
    down, up, merged = row_tables()
    for matrix in (down, up):
        high, low = split_parts(matrix)
        sums.append(np.concatenate([high, high, low], 1))
    for level in range(3):
        high, low = split_parts(merged[level])
        pan_rows.append(np.concatenate([high, high, low], 1))
    return np.stack(ms_rows), ms_cols, pan_cols, np.stack(pan_rows), np.stack(sums)


def parts_of(x):
    high = x.astype(jnp.bfloat16)
    low = (x - high.astype(jnp.float32)).astype(jnp.bfloat16)
    return high, low


def rolled(tiles, beside):
    left = lax.broadcasted_iota(jnp.int32, beside.shape, 1) < 64
    turned = [pltpu.roll(tile, 64, 1) for tile in tiles]
    firsts, seconds = [beside] + turned, turned + [beside]
    return [jnp.where(left, one, two) for one, two in zip(firsts, seconds)]


def spread(
    nr, nc,
    ms_hbm, pan_hbm, gains_hbm, ms_rows_hbm, ms_cols_hbm, pan_cols_hbm, pan_rows_hbm, sums_hbm,
    terms, ysplit, ms_rows,
    ms_own, stage, ostage, mbuf, obuf, pan_own, psums, pan_above_below, pstage, precv, cstage, crecv,
    ms_cols, pan_cols, pan_rows, sums,
    pan_split, zbuf, qbuf, xbuf,
    gains, load_sems, ms_recv, pan_recv, send_sems,
):
    r, c = lax.axis_index("row"), lax.axis_index("col")
    half = nc // 2
    row_of = {d: lax.rem(r + d + nr, nr) for d in (-1, 0, 1)}
    side, place = c // half, lax.rem(c, half)
    halves = [lax.rem(side + a, 2) * half for a in range(2)]
    col_of = {
        (a, k): halves[a] + lax.rem(place + k, half) for a in range(2) for k in range(half)
    }

    ms_load = pltpu.make_async_copy(ms_hbm.at[0], ms_own, load_sems.at[0])
    pan_load = pltpu.make_async_copy(pan_hbm, pan_own, load_sems.at[1])
    sums_load = pltpu.make_async_copy(sums_hbm, sums, load_sems.at[7])
    ms_load.start()
    pan_load.start()
    sums_load.start()

    odd = lax.rem(r, 2)
    inner = lax.rem(r + 1 - 2 * odd + nr, nr)
    outer = lax.rem(r - 1 + 2 * odd + nr, nr)

    barrier = pltpu.get_barrier_semaphore()
    for col in col_of.values():
        pl.semaphore_signal(barrier, inc=1, device_id=(outer, col), device_id_type=MESH)
    for at, col in col_of.items():
        if at != (0, 0):
            pl.semaphore_signal(barrier, inc=1, device_id=(r, col), device_id_type=MESH)
    for k in (0, 1, nc - 1):
        pl.semaphore_signal(
            barrier, inc=1, device_id=(inner, lax.rem(c + k, nc)), device_id_type=MESH
        )

    table_loads = [
        pltpu.make_async_copy(source, target, load_sems.at[2 + i])
        for i, (source, target) in enumerate(
            (
                (pan_cols_hbm, pan_cols),
                (pan_rows_hbm, pan_rows),
                (gains_hbm, gains),
                (ms_cols_hbm, ms_cols),
                (ms_rows_hbm.at[odd], ms_rows),
            )
        )
    ]
    for load in table_loads:
        load.start()

    lane = lax.broadcasted_iota(jnp.int32, (8, 128), 1)
    sublane = lax.broadcasted_iota(jnp.int32, (8, 128), 0)

    ms_load.wait()
    for dest in range(nc):
        tile = slice(128 * dest, 128 * dest + 128)
        before = (dest - 1) % nc
        after = (dest + 1) % nc
        stage[dest, 0:16] = ms_own[0:16, tile]
        stage[dest, 24:40] = ms_own[16:32, tile]
        rim = None
        for q in range(4):
            rows = slice(8 * q, 8 * q + 8)
            both = jnp.where(
                lane < 64,
                ms_own[rows, 128 * after : 128 * after + 128],
                ms_own[rows, 128 * before : 128 * before + 128],
            )
            both = pltpu.roll(both, (16 + 32 * q) % 128, 1)
            rim = both if rim is None else jnp.where(lane < 32 * q, rim, both)
        stage[dest, 16:24] = rim

    for way in range(2):

        @pl.when(odd == way)
        def _():
            for dest in range(nc):
                tile = slice(128 * dest, 128 * dest + 128)
                if way:
                    upper, lower = ms_own[16:24, tile], ms_own[24:32, tile]
                else:
                    upper = pltpu.roll(ms_own[0:8, tile], 3, 0)
                    lower = jnp.where(sublane < 3, upper, pltpu.roll(ms_own[8:16, tile], 3, 0))
                rim = stage[dest, 16:24]
                for i, count, at, first, last in RIM_PIECES:
                    row = i + 19 * way
                    while count:
                        q, sub = row // 8, row % 8
                        now = min(count, 8 - sub)
                        moved = pltpu.roll(rim, (at[0] - sub) % 8, 0)
                        moved = pltpu.roll(moved, (at[1] - 32 * q - first) % 128, 1)
                        inside = (sublane >= at[0]) & (sublane < at[0] + now)
                        inside &= (lane >= at[1]) & (lane < at[1] + last - first)
                        upper = jnp.where(inside, moved, upper)
                        row, count, at = row + now, count - now, (at[0] + now, at[1])
                ostage[dest, 0:8] = upper
                ostage[dest, 8:16] = lower

    pl.semaphore_wait(barrier, 2 * nc + 2)

    def remote(source, target, send_sem, recv_sem, row, col):
        return pltpu.make_async_remote_copy(
            src_ref=source,
            dst_ref=target,
            send_sem=send_sem,
            recv_sem=recv_sem,
            device_id=(row, col),
            device_id_type=MESH,
        )

    def rows_of(first, count):
        return pl.ds(pl.multiple_of(first, 8), count)

    for a in (1, 0):
        for k in range(half):
            if a or k:
                col = col_of[a, k]
                remote(
                    stage.at[col], mbuf.at[c, 0:40], send_sems.at[0], ms_recv.at[0, a], r, col
                ).start()
    mbuf[c, 0:40] = stage[c]

    pan_load.wait()
    sums_load.wait()
    for way, rows in ((0, slice(ROWS - PAN_SENT, ROWS)), (1, slice(0, PAN_SENT))):
        high, low = parts_of(pan_own[rows])
        psums[way] = jnp.dot(
            sums[way], jnp.concatenate([high, low, high], 0), preferred_element_type=jnp.float32
        )
    for source, at in ((pan_own, pstage), (psums.at[0], cstage.at[0]), (psums.at[1], cstage.at[1])):
        half_rows = source.shape[0] // 2
        left = lax.broadcasted_iota(jnp.int32, (half_rows, 128), 1) < 64
        last, first = source[:, 384:512], source[:, 0:128]
        at[0] = jnp.where(left, pltpu.roll(last[:half_rows], 64, 1), last[half_rows:])
        at[1] = jnp.where(left, first[:half_rows], pltpu.roll(first[half_rows:], 64, 1))

    def send_outer(a):
        for k in range(half):
            col = col_of[a, k]
            remote(
                ostage.at[col], obuf.at[c], send_sems.at[1], ms_recv.at[1, a], outer, col
            ).start()

    send_outer(1)
    for way, d in ((0, 1), (1, -1)):
        remote(
            psums.at[way], pan_above_below.at[way],
            send_sems.at[3], pan_recv.at[0], row_of[d], c,
        ).start()
    for side_at, k in ((0, 1), (1, nc - 1)):
        beside = lax.rem(c + k, nc)
        remote(
            pstage.at[side_at], precv.at[side_at], send_sems.at[4], pan_recv.at[1], r, beside
        ).start()
        for way, d in ((0, 1), (1, -1)):
            remote(
                cstage.at[way, side_at], crecv.at[way, side_at],
                send_sems.at[5], pan_recv.at[2], row_of[d], beside,
            ).start()
    send_outer(0)

    for a in (0, 1):
        arrived = mbuf.at[0 : half - 1 + a, 0:40]
        remote(arrived, arrived, send_sems.at[0], ms_recv.at[0, a], r, col_of[0, 1]).wait_recv()
        bands = pl.ds(halves[a], half)
        remote(
            mbuf.at[bands, rows_of(16 - 16 * odd, 24)], mbuf.at[bands, 40:64],
            send_sems.at[2], ms_recv.at[2, a], inner, c,
        ).start()

    def unpacked(packed):
        left = lax.broadcasted_iota(jnp.int32, packed.shape[1:], 1) < 64
        one, two = packed[0], packed[1]
        return jnp.concatenate(
            [
                jnp.where(left, one, pltpu.roll(two, 64, 1)),
                jnp.where(left, pltpu.roll(one, 64, 1), two),
            ],
            0,
        )

    def pan_columns(rows, count, tiles, ends):
        for t, tile in enumerate(rolled(tiles, ends)):
            for part, value in enumerate(parts_of(tile)):
                pan_split[part, rows : rows + count, 128 * t : 128 * t + 128] = value
        for j in range(4):
            window = slice(128 * j, 128 * j + 256)
            high, low = (pan_split[part, rows : rows + count, window] for part in range(2))
            z = jnp.dot(
                jnp.concatenate([high, low, high], 1),
                pan_cols[...],
                preferred_element_type=jnp.float32,
            )
            for level in range(3):
                high, low = parts_of(z[:, 128 * level : 128 * level + 128])
                for at, part in ((0, high), (1, low), (2, high)):
                    first = PAN_EXT * at + rows
                    zbuf[level, first : first + count, 128 * j : 128 * j + 128] = part

    def ms_columns(bands, at):
        high, low = parts_of(xbuf[0 : 32 * len(bands)])
        y = jnp.dot(
            jnp.concatenate([high, low, high], 1), ms_cols[...], preferred_element_type=jnp.float32
        )
        high, low = parts_of(y)
        for i, b in enumerate(bands):
            ysplit[b, at : at + 32] = high[32 * i : 32 * i + 32]
            ysplit[b, 64 + at : 96 + at] = low[32 * i : 32 * i + 32]

    for b in range(BANDS):
        rim = mbuf[b, 16:24]
        for q, first in enumerate((0, 8, 24, 32)):
            rows = slice(32 * b + 8 * q, 32 * b + 8 * q + 8)
            xbuf[rows, 0:128] = mbuf[b, first : first + 8]
            xbuf[rows, 128:256] = pltpu.roll(rim, (128 - 32 * q) % 128, 1)
    for load in table_loads:
        load.wait()
    ms_columns(range(BANDS), 0)

    remote(pstage, precv, send_sems.at[4], pan_recv.at[1], r, col_of[0, 1]).wait_recv()
    tiles = [pan_own[:, 128 * t : 128 * t + 128] for t in range(4)]
    pan_columns(0, ROWS, tiles, unpacked(precv))
    remote(psums, psums, send_sems.at[3], pan_recv.at[0], row_of[1], c).wait_recv()
    remote(cstage, crecv, send_sems.at[5], pan_recv.at[2], row_of[1], c).wait_recv()
    tiles = [
        jnp.concatenate([pan_above_below[way, :, 128 * t : 128 * t + 128] for way in range(2)], 0)
        for t in range(4)
    ]
    ends = jnp.concatenate([unpacked(crecv.at[0]), unpacked(crecv.at[1])], 0)
    pan_columns(ROWS, 2 * PAN_RIM, tiles, ends)
    for level in range(3):
        qbuf[level] = jnp.dot(pan_rows[level], zbuf[level], preferred_element_type=jnp.float32)

    def weigh(step, carry):
        rows = pl.ds(pl.multiple_of(8 * step, 8), 8)
        fields = [pan_own[rows, :]] + [qbuf[level, rows, :] for level in range(3)]
        for b in range(BANDS):
            g1, g2, g3 = gains[0, b], gains[1, b], gains[2, b]
            terms[b, rows, :] = (
                g1 * fields[0] + (g2 - g1) * fields[1] + (g3 - g2) * fields[2] - g3 * fields[3]
            )
        return carry

    lax.fori_loop(0, ROWS // 8, weigh, 0)

    for a in range(2):
        arrived = mbuf.at[0:half, 0:24]
        remote(arrived, arrived, send_sems.at[2], ms_recv.at[2, a], inner, c).wait_recv()
        arrived = obuf.at[0:half]
        remote(arrived, arrived, send_sems.at[1], ms_recv.at[1, a], outer, c).wait_recv()
        bands = [halves[a] + k for k in range(half)]
        for k, b in enumerate(bands):
            rim = mbuf[b, rows_of(56 - 16 * odd, 8)]
            for q in range(2):
                rows = slice(32 * k + 8 * q, 32 * k + 8 * q + 8)
                xbuf[rows, 0:128] = mbuf[b, rows_of(40 + 8 * odd + 8 * q, 8)]
                at = 32 * q + 64 * odd
                xbuf[rows, 128:256] = pltpu.roll(rim, lax.rem(128 - at, 128), 1)
            upper, lower = obuf[b, 0:8], obuf[b, 8:16]
            rims = [upper, lower]
            for i, count, at, first, last in RIM_PIECES:
                moved = pltpu.roll(upper, (i + 3 - at[0]) % 8, 0)
                moved = pltpu.roll(moved, (first - at[1]) % 128, 1)
                for v in range(2):
                    low, high = i + 3 - 8 * v, i + 3 + count - 8 * v
                    if low < 8 and high > 0:
                        inside = (sublane >= low) & (sublane < high)
                        if last - first < 26:
                            inside &= (lane >= first) & (lane < last)
                        rims[v] = jnp.where(inside, moved, rims[v])
            for v, main in enumerate((upper, lower)):
                rows = slice(32 * k + 16 + 8 * v, 32 * k + 24 + 8 * v)
                xbuf[rows, 0:128] = main
                xbuf[rows, 128:256] = rims[v]
        ms_columns(bands, 32)

    sent = (stage.at[0 : nc - 1], ostage, mbuf.at[:, 0:24], psums, pstage, cstage)
    for at, source in enumerate(sent):
        remote(source, source, send_sems.at[at], pan_recv.at[0], inner, c).wait_send()


def finish(terms, ysplit, ms_rows, out_hbm, result, sem):
    for b in range(BANDS):
        high = ysplit[b, 0:64]
        column = jnp.concatenate([high, ysplit[b, 64:128], high], 0)
        result[b] = terms[b] + jnp.dot(ms_rows[...], column, preferred_element_type=jnp.float32)
        pltpu.make_async_copy(result.at[b], out_hbm.at[b], sem).start()
    pltpu.make_async_copy(result, out_hbm, sem).wait()


def in_hbm(x):
    return pltpu.with_memory_space_constraint(x, pltpu.HBM)


def on_device(nr, nc, tables, ms, pan, gains):
    f32 = jnp.float32
    bf16 = jnp.bfloat16
    hbm = pl.BlockSpec(memory_space=pl.ANY)
    vmem = pl.BlockSpec(memory_space=pltpu.VMEM)
    shared = pl.pallas_call(
        functools.partial(spread, nr, nc),
        out_shape=[
            pltpu.VMEM((BANDS, ROWS, COLS), f32),
            pltpu.VMEM((BANDS, 128, COLS), bf16),
            pltpu.VMEM(tables[0].shape[1:], bf16),
        ],
        in_specs=[hbm] * 8,
        out_specs=[vmem] * 3,
        scratch_shapes=[
            pltpu.VMEM((LROWS, nc * LCOLS), f32),
            pltpu.VMEM((nc, 40, 128), f32),
            pltpu.VMEM((nc, 16, 128), f32),
            pltpu.VMEM((BANDS, 64, 128), f32),
            pltpu.VMEM((BANDS, 16, 128), f32),
            pltpu.VMEM((ROWS, COLS), f32),
            pltpu.VMEM((2, PAN_RIM, COLS), f32),
            pltpu.VMEM((2, PAN_RIM, COLS), f32),
            pltpu.VMEM((2, 64, 128), f32),
            pltpu.VMEM((2, 64, 128), f32),
            pltpu.VMEM((2, 2, 16, 128), f32),
            pltpu.VMEM((2, 2, 16, 128), f32),
            *[pltpu.VMEM(table.shape, bf16) for table in tables[1:]],
            pltpu.VMEM((2, PAN_EXT, COLS + 128), bf16),
            pltpu.VMEM((3, 3 * PAN_EXT, COLS), bf16),
            pltpu.VMEM((3, ROWS, COLS), f32),
            pltpu.VMEM((BANDS * 32, 256), f32),
            pltpu.SMEM((3, BANDS), f32),
            pltpu.SemaphoreType.DMA((8,)),
            pltpu.SemaphoreType.DMA((3, 2)),
            pltpu.SemaphoreType.DMA((3,)),
            pltpu.SemaphoreType.DMA((6,)),
        ],
        compiler_params=pltpu.CompilerParams(
            collective_id=0, has_side_effects=True, vmem_limit_bytes=32 * 1024 * 1024
        ),
    )(in_hbm(ms), in_hbm(pan), in_hbm(gains.T), *[in_hbm(jnp.asarray(table)) for table in tables])
    return pl.pallas_call(
        finish,
        out_shape=jax.ShapeDtypeStruct((BANDS, ROWS, COLS), f32),
        in_specs=[vmem] * 3,
        out_specs=hbm,
        scratch_shapes=[pltpu.VMEM((BANDS, ROWS, COLS), f32), pltpu.SemaphoreType.DMA],
        compiler_params=pltpu.CompilerParams(vmem_limit_bytes=16 * 1024 * 1024),
    )(*shared)


def solution(mesh):
    tables = make_tables()
    nr, nc = mesh.shape["row"], mesh.shape["col"]
    return jax.shard_map(
        functools.partial(on_device, nr, nc, tables),
        mesh=mesh,
        in_specs=(P("col", "row", None), P("row", "col"), P()),
        out_specs=P(None, "row", "col"),
        check_vma=False,
    )
```

```python
import functools
import math

import jax
import jax.numpy as jnp
import ml_dtypes
import numpy as np
from jax import lax
from jax.experimental import pallas as pl
from jax.experimental.pallas import tpu as pltpu
from jax.sharding import PartitionSpec as P

MESH = pl.DeviceIdType.MESH
BF16 = ml_dtypes.bfloat16

TAPS = [
    0.2303778133088964,
    0.7148465705529154,
    0.6308807679298587,
    -0.0279837694168599,
    -0.1870348117190931,
    0.0308413818355607,
    0.0328830116668852,
    -0.0105974017850690,
]

ROWS, COLS = 128, 512
LROWS, LCOLS = 32, 128
PAN_RIM = 32
PAN_SENT = 48
PAN_EXT = ROWS + 2 * PAN_RIM
MS_RIM = 16
BANDS = 8

RIM_PIECES = [(3 * j, 3, (0, 26 * j), 3, 29) for j in range(4)]
RIM_PIECES += [(12, 1, (0, 104), 3, 16), (12, 1, (1, 104), 16, 29)]


def windows(level):
    found = []
    for tree in range(2):
        taps = TAPS if tree == 0 else TAPS[::-1]
        cascade, shift = [1.0], 0
        for lev in range(level):
            longer = [0.0] * (len(cascade) + 7 * 2**lev)
            for i, value in enumerate(cascade):
                for j, tap in enumerate(taps):
                    longer[i + j * 2**lev] += value * tap
            cascade, shift = longer, shift + (3 + tree) * 2**lev
        found.append((2**level, shift, cascade))
    return found


def projection(level):
    rows = [{} for _ in range(8)]
    for step, shift, cascade in windows(level):
        for m in range(8):
            for k in range(-64, 64):
                at = m - step * k + shift
                if 0 <= at < len(cascade):
                    for i, value in enumerate(cascade):
                        offset = step * k - shift + i - m
                        rows[m][offset] = rows[m].get(offset, 0.0) + 0.5 * cascade[at] * value
    return rows


def cubic_weight(distance):
    magnitude = abs(distance)
    if magnitude <= 1.0:
        return 1.5 * magnitude**3 - 2.5 * magnitude**2 + 1.0
    if magnitude < 2.0:
        return -0.5 * magnitude**3 + 2.5 * magnitude**2 - 4.0 * magnitude + 2.0
    return 0.0


def upsampled_projection():
    rows = [{} for _ in range(8)]
    for m, weights in enumerate(projection(3)):
        for offset in sorted(weights):
            position = (m + offset + 0.5) / 4.0 - 0.5
            floor = math.floor(position)
            for low in range(floor - 1, floor + 3):
                term = weights[offset] * cubic_weight(position - low)
                rows[m][low] = rows[m].get(low, 0.0) + term
    return rows


def split_parts(matrix):
    high = matrix.astype(np.float32).astype(BF16)
    low = (matrix - high.astype(np.float64)).astype(np.float32).astype(BF16)
    return high, low


def pan_matrix(level, outs, ins, start):
    matrix = np.zeros((outs, ins))
    rows = projection(level)
    for m in range(outs):
        for offset, weight in rows[m % 8].items():
            if 0 <= m + offset - start < ins:
                matrix[m, m + offset - start] = weight
    return matrix


def straddling(edge):
    found = []
    for level in (1, 2, 3):
        for step, shift, cascade in windows(level):
            for k in range(-64, 128):
                first = step * k - shift
                if first < edge < first + len(cascade):
                    found.append((level, first, cascade))
    return found


def row_tables():
    above, below = straddling(0), straddling(ROWS)
    down = np.zeros((PAN_RIM, PAN_SENT))
    up = np.zeros((PAN_RIM, PAN_SENT))
    merged = np.zeros((3, ROWS, PAN_EXT))
    for level in (1, 2, 3):
        merged[level - 1, :, :ROWS] = pan_matrix(level, ROWS, ROWS, 0)
    for at, (level, first, cascade) in enumerate(above):
        for i, weight in enumerate(cascade):
            if first + i < 0:
                down[at, first + i + PAN_SENT] = weight
            else:
                merged[level - 1, first + i, ROWS + at] = 0.5 * weight
    for at, (level, first, cascade) in enumerate(below):
        for i, weight in enumerate(cascade):
            if first + i >= ROWS:
                up[at, first + i - ROWS] = weight
            else:
                merged[level - 1, first + i, ROWS + PAN_RIM + at] = 0.5 * weight
    return down, up, merged


def ms_matrix(outs, ins, lows):
    place = {low: at for at, low in lows}
    matrix = np.zeros((outs, ins))
    rows = upsampled_projection()
    for m in range(outs):
        for low, weight in rows[m % 8].items():
            matrix[m, place[low + 2 * (m // 8)]] = weight
    return matrix


def make_tables():
    ms_rows = []
    for odd in (0, 1):
        inner, outer = (-16, 32) if odd else (32, -13)
        lows = [(i, i) for i in range(LROWS)]
        lows += [(LROWS + i, inner + i) for i in range(16)]
        lows += [(LROWS + 19 + i, outer + i) for i in range(13)]
        high, low = split_parts(ms_matrix(ROWS, 64, lows))
        ms_rows.append(np.concatenate([high, high, low], 1))
    lows = [(i, i) for i in range(LCOLS)]
    lows += [(LCOLS + i, i - MS_RIM) for i in range(MS_RIM)]
    lows += [(LCOLS + MS_RIM + i, LCOLS + i) for i in range(MS_RIM)]
    high, low = split_parts(ms_matrix(COLS, 256, lows).T)
    ms_cols = np.concatenate([high, high, low], 0)
    matrix = np.concatenate([pan_matrix(level, 128, 256, -64) for level in (1, 2, 3)], 0).T
    high, low = split_parts(matrix)
    pan_cols = np.concatenate([high, high, low], 0)
    sums, pan_rows = [], []
    down, up, merged = row_tables()
    for matrix in (down, up):
        high, low = split_parts(matrix)
        sums.append(np.concatenate([high, high, low], 1))
    for level in range(3):
        high, low = split_parts(merged[level])
        pan_rows.append(np.concatenate([high, high, low], 1))
    return np.stack(ms_rows), ms_cols, pan_cols, np.stack(pan_rows), np.stack(sums)


def parts_of(x):
    high = x.astype(jnp.bfloat16)
    low = (x - high.astype(jnp.float32)).astype(jnp.bfloat16)
    return high, low


def rolled(tiles, beside):
    left = lax.broadcasted_iota(jnp.int32, beside.shape, 1) < 64
    turned = [pltpu.roll(tile, 64, 1) for tile in tiles]
    firsts, seconds = [beside] + turned, turned + [beside]
    return [jnp.where(left, one, two) for one, two in zip(firsts, seconds)]


def column_parts(x, ms_cols):
    high, low = parts_of(x)
    y = jnp.dot(
        jnp.concatenate([high, low, high], 1), ms_cols[...], preferred_element_type=jnp.float32
    )
    return parts_of(y)


def spread(
    nr, nc,
    ms_hbm, pan_hbm, gains_hbm, ms_rows_hbm, ms_cols_hbm, pan_cols_hbm, pan_rows_hbm, sums_hbm,
    pan_own, qbuf, weights, ysplit, xlast, ms_cols, ms_rows,
    ms_own, stage, ostage, mbuf, obuf, psums, pan_above_below, pstage, precv, cstage, crecv,
    pan_cols, pan_rows, sums,
    pan_split, zbuf, xbuf,
    gains, load_sems, ms_recv, pan_recv, send_sems,
):
    r, c = lax.axis_index("row"), lax.axis_index("col")
    half = nc // 2
    row_of = {d: lax.rem(r + d + nr, nr) for d in (-1, 0, 1)}
    side, place = c // half, lax.rem(c, half)
    halves = [lax.rem(side + a, 2) * half for a in range(2)]
    col_of = {
        (a, k): halves[a] + lax.rem(place + k, half) for a in range(2) for k in range(half)
    }

    ms_load = pltpu.make_async_copy(ms_hbm.at[0], ms_own, load_sems.at[0])
    pan_load = pltpu.make_async_copy(pan_hbm, pan_own, load_sems.at[1])
    sums_load = pltpu.make_async_copy(sums_hbm, sums, load_sems.at[7])
    ms_load.start()
    pan_load.start()
    sums_load.start()

    odd = lax.rem(r, 2)
    inner = lax.rem(r + 1 - 2 * odd + nr, nr)
    outer = lax.rem(r - 1 + 2 * odd + nr, nr)

    barrier = pltpu.get_barrier_semaphore()
    for col in col_of.values():
        pl.semaphore_signal(barrier, inc=1, device_id=(outer, col), device_id_type=MESH)
    for at, col in col_of.items():
        if at != (0, 0):
            pl.semaphore_signal(barrier, inc=1, device_id=(r, col), device_id_type=MESH)
    for k in (0, 1, nc - 1):
        pl.semaphore_signal(
            barrier, inc=1, device_id=(inner, lax.rem(c + k, nc)), device_id_type=MESH
        )

    table_loads = [
        pltpu.make_async_copy(source, target, load_sems.at[2 + i])
        for i, (source, target) in enumerate(
            (
                (pan_cols_hbm, pan_cols),
                (pan_rows_hbm, pan_rows),
                (gains_hbm, gains),
                (ms_cols_hbm, ms_cols),
                (ms_rows_hbm.at[odd], ms_rows),
            )
        )
    ]
    for load in table_loads:
        load.start()

    lane = lax.broadcasted_iota(jnp.int32, (8, 128), 1)
    sublane = lax.broadcasted_iota(jnp.int32, (8, 128), 0)

    ms_load.wait()
    for dest in range(nc):
        tile = slice(128 * dest, 128 * dest + 128)
        before = (dest - 1) % nc
        after = (dest + 1) % nc
        stage[dest, 0:16] = ms_own[0:16, tile]
        stage[dest, 24:40] = ms_own[16:32, tile]
        rim = None
        for q in range(4):
            rows = slice(8 * q, 8 * q + 8)
            both = jnp.where(
                lane < 64,
                ms_own[rows, 128 * after : 128 * after + 128],
                ms_own[rows, 128 * before : 128 * before + 128],
            )
            both = pltpu.roll(both, (16 + 32 * q) % 128, 1)
            rim = both if rim is None else jnp.where(lane < 32 * q, rim, both)
        stage[dest, 16:24] = rim

    for way in range(2):

        @pl.when(odd == way)
        def _():
            for dest in range(nc):
                tile = slice(128 * dest, 128 * dest + 128)
                if way:
                    upper, lower = ms_own[16:24, tile], ms_own[24:32, tile]
                else:
                    upper = pltpu.roll(ms_own[0:8, tile], 3, 0)
                    lower = jnp.where(sublane < 3, upper, pltpu.roll(ms_own[8:16, tile], 3, 0))
                rim = stage[dest, 16:24]
                for i, count, at, first, last in RIM_PIECES:
                    row = i + 19 * way
                    while count:
                        q, sub = row // 8, row % 8
                        now = min(count, 8 - sub)
                        moved = pltpu.roll(rim, (at[0] - sub) % 8, 0)
                        moved = pltpu.roll(moved, (at[1] - 32 * q - first) % 128, 1)
                        inside = (sublane >= at[0]) & (sublane < at[0] + now)
                        inside &= (lane >= at[1]) & (lane < at[1] + last - first)
                        upper = jnp.where(inside, moved, upper)
                        row, count, at = row + now, count - now, (at[0] + now, at[1])
                ostage[dest, 0:8] = upper
                ostage[dest, 8:16] = lower

    pl.semaphore_wait(barrier, 2 * nc + 2)

    def remote(source, target, send_sem, recv_sem, row, col):
        return pltpu.make_async_remote_copy(
            src_ref=source,
            dst_ref=target,
            send_sem=send_sem,
            recv_sem=recv_sem,
            device_id=(row, col),
            device_id_type=MESH,
        )

    def rows_of(first, count):
        return pl.ds(pl.multiple_of(first, 8), count)

    for a in (1, 0):
        for k in range(half):
            if a or k:
                col = col_of[a, k]
                remote(
                    stage.at[col], mbuf.at[c, 0:40], send_sems.at[0], ms_recv.at[0, a], r, col
                ).start()
    mbuf[c, 0:40] = stage[c]

    pan_load.wait()
    sums_load.wait()
    for way, rows in ((0, slice(ROWS - PAN_SENT, ROWS)), (1, slice(0, PAN_SENT))):
        high, low = parts_of(pan_own[rows])
        psums[way] = jnp.dot(
            sums[way], jnp.concatenate([high, low, high], 0), preferred_element_type=jnp.float32
        )
    for source, at in ((pan_own, pstage), (psums.at[0], cstage.at[0]), (psums.at[1], cstage.at[1])):
        half_rows = source.shape[0] // 2
        left = lax.broadcasted_iota(jnp.int32, (half_rows, 128), 1) < 64
        last, first = source[:, 384:512], source[:, 0:128]
        at[0] = jnp.where(left, pltpu.roll(last[:half_rows], 64, 1), last[half_rows:])
        at[1] = jnp.where(left, first[:half_rows], pltpu.roll(first[half_rows:], 64, 1))

    def send_outer(a):
        for k in range(half):
            col = col_of[a, k]
            remote(
                ostage.at[col], obuf.at[c], send_sems.at[1], ms_recv.at[1, a], outer, col
            ).start()

    send_outer(1)
    for way, d in ((0, 1), (1, -1)):
        remote(
            psums.at[way], pan_above_below.at[way],
            send_sems.at[3], pan_recv.at[0], row_of[d], c,
        ).start()
    for side_at, k in ((0, 1), (1, nc - 1)):
        beside = lax.rem(c + k, nc)
        remote(
            pstage.at[side_at], precv.at[side_at], send_sems.at[4], pan_recv.at[1], r, beside
        ).start()
        for way, d in ((0, 1), (1, -1)):
            remote(
                cstage.at[way, side_at], crecv.at[way, side_at],
                send_sems.at[5], pan_recv.at[2], row_of[d], beside,
            ).start()
    send_outer(0)

    for a in (0, 1):
        arrived = mbuf.at[0 : half - 1 + a, 0:40]
        remote(arrived, arrived, send_sems.at[0], ms_recv.at[0, a], r, col_of[0, 1]).wait_recv()
        bands = pl.ds(halves[a], half)
        remote(
            mbuf.at[bands, rows_of(16 - 16 * odd, 24)], mbuf.at[bands, 40:64],
            send_sems.at[2], ms_recv.at[2, a], inner, c,
        ).start()

    def unpacked(packed):
        left = lax.broadcasted_iota(jnp.int32, packed.shape[1:], 1) < 64
        one, two = packed[0], packed[1]
        return jnp.concatenate(
            [
                jnp.where(left, one, pltpu.roll(two, 64, 1)),
                jnp.where(left, pltpu.roll(one, 64, 1), two),
            ],
            0,
        )

    def pan_columns(rows, count, tiles, ends):
        for t, tile in enumerate(rolled(tiles, ends)):
            for part, value in enumerate(parts_of(tile)):
                pan_split[part, rows : rows + count, 128 * t : 128 * t + 128] = value
        for j in range(4):
            window = slice(128 * j, 128 * j + 256)
            high, low = (pan_split[part, rows : rows + count, window] for part in range(2))
            z = jnp.dot(
                jnp.concatenate([high, low, high], 1),
                pan_cols[...],
                preferred_element_type=jnp.float32,
            )
            for level in range(3):
                high, low = parts_of(z[:, 128 * level : 128 * level + 128])
                for at, part in ((0, high), (1, low), (2, high)):
                    first = PAN_EXT * at + rows
                    zbuf[level, first : first + count, 128 * j : 128 * j + 128] = part

    def ms_columns(bands, at):
        high, low = column_parts(xbuf[0 : 32 * len(bands)], ms_cols)
        for i, b in enumerate(bands):
            ysplit[b, at : at + 32] = high[32 * i : 32 * i + 32]
            ysplit[b, 64 + at : 96 + at] = low[32 * i : 32 * i + 32]

    for b in range(BANDS):
        rim = mbuf[b, 16:24]
        for q, first in enumerate((0, 8, 24, 32)):
            rows = slice(32 * b + 8 * q, 32 * b + 8 * q + 8)
            xbuf[rows, 0:128] = mbuf[b, first : first + 8]
            xbuf[rows, 128:256] = pltpu.roll(rim, (128 - 32 * q) % 128, 1)
    for load in table_loads:
        load.wait()
    ms_columns(range(BANDS), 0)

    remote(pstage, precv, send_sems.at[4], pan_recv.at[1], r, col_of[0, 1]).wait_recv()
    tiles = [pan_own[:, 128 * t : 128 * t + 128] for t in range(4)]
    pan_columns(0, ROWS, tiles, unpacked(precv))
    remote(psums, psums, send_sems.at[3], pan_recv.at[0], row_of[1], c).wait_recv()
    remote(cstage, crecv, send_sems.at[5], pan_recv.at[2], row_of[1], c).wait_recv()
    tiles = [
        jnp.concatenate([pan_above_below[way, :, 128 * t : 128 * t + 128] for way in range(2)], 0)
        for t in range(4)
    ]
    ends = jnp.concatenate([unpacked(crecv.at[0]), unpacked(crecv.at[1])], 0)
    pan_columns(ROWS, 2 * PAN_RIM, tiles, ends)
    for level in range(3):
        qbuf[level] = jnp.dot(pan_rows[level], zbuf[level], preferred_element_type=jnp.float32)

    for b in range(BANDS):
        g1, g2, g3 = gains[0, b], gains[1, b], gains[2, b]
        for at, weight in enumerate((g1, g2 - g1, g3 - g2, -g3)):
            weights[4 * b + at : 4 * b + at + 1] = jnp.full((1, COLS), weight, jnp.float32)

    for a in range(2):
        arrived = mbuf.at[0:half, 0:24]
        remote(arrived, arrived, send_sems.at[2], ms_recv.at[2, a], inner, c).wait_recv()
        arrived = obuf.at[0:half]
        remote(arrived, arrived, send_sems.at[1], ms_recv.at[1, a], outer, c).wait_recv()
        bands = [halves[a] + k for k in range(half)]
        target = xlast if a else xbuf
        for k, b in enumerate(bands):
            rim = mbuf[b, rows_of(56 - 16 * odd, 8)]
            for q in range(2):
                rows = slice(32 * k + 8 * q, 32 * k + 8 * q + 8)
                target[rows, 0:128] = mbuf[b, rows_of(40 + 8 * odd + 8 * q, 8)]
                at = 32 * q + 64 * odd
                target[rows, 128:256] = pltpu.roll(rim, lax.rem(128 - at, 128), 1)
            upper, lower = obuf[b, 0:8], obuf[b, 8:16]
            rims = [upper, lower]
            for i, count, at, first, last in RIM_PIECES:
                moved = pltpu.roll(upper, (i + 3 - at[0]) % 8, 0)
                moved = pltpu.roll(moved, (first - at[1]) % 128, 1)
                for v in range(2):
                    low, high = i + 3 - 8 * v, i + 3 + count - 8 * v
                    if low < 8 and high > 0:
                        inside = (sublane >= low) & (sublane < high)
                        if last - first < 26:
                            inside &= (lane >= first) & (lane < last)
                        rims[v] = jnp.where(inside, moved, rims[v])
            for v, main in enumerate((upper, lower)):
                rows = slice(32 * k + 16 + 8 * v, 32 * k + 24 + 8 * v)
                target[rows, 0:128] = main
                target[rows, 128:256] = rims[v]
        if a == 0:
            ms_columns(bands, 32)

    sent = (stage.at[0 : nc - 1], ostage, mbuf.at[:, 0:24], psums, pstage, cstage)
    for at, source in enumerate(sent):
        remote(source, source, send_sems.at[at], pan_recv.at[0], inner, c).wait_send()


def finish(nc, pan, qbuf, weights, ysplit, xlast, ms_cols, ms_rows, out_hbm, result, sem):
    half = nc // 2
    side = lax.axis_index("col") // half
    for a in range(2):
        first = lax.rem(side + a, 2) * half
        if a:
            rim_high, rim_low = column_parts(xlast[...], ms_cols)
        for k in range(half):
            b = first + k
            if a:
                rows = slice(32 * k, 32 * k + 32)
                high = jnp.concatenate([ysplit[b, 0:32], rim_high[rows]], 0)
                low = jnp.concatenate([ysplit[b, 64:96], rim_low[rows]], 0)
            else:
                high, low = ysplit[b, 0:64], ysplit[b, 64:128]
            total = jnp.dot(
                ms_rows[...],
                jnp.concatenate([high, low, high], 0),
                preferred_element_type=jnp.float32,
            )
            for at, field in enumerate((pan, qbuf.at[0], qbuf.at[1], qbuf.at[2])):
                total += weights[pl.ds(4 * b + at, 1)] * field[...]
            result[b] = total
            pltpu.make_async_copy(result.at[b], out_hbm.at[b], sem).start()
    pltpu.make_async_copy(result, out_hbm, sem).wait()


def in_hbm(x):
    return pltpu.with_memory_space_constraint(x, pltpu.HBM)


def on_device(nr, nc, tables, ms, pan, gains):
    f32 = jnp.float32
    bf16 = jnp.bfloat16
    hbm = pl.BlockSpec(memory_space=pl.ANY)
    vmem = pl.BlockSpec(memory_space=pltpu.VMEM)
    shared = pl.pallas_call(
        functools.partial(spread, nr, nc),
        out_shape=[
            pltpu.VMEM((ROWS, COLS), f32),
            pltpu.VMEM((3, ROWS, COLS), f32),
            pltpu.VMEM((4 * BANDS, COLS), f32),
            pltpu.VMEM((BANDS, 128, COLS), bf16),
            pltpu.VMEM((BANDS // 2 * 32, 256), f32),
            pltpu.VMEM(tables[1].shape, bf16),
            pltpu.VMEM(tables[0].shape[1:], bf16),
        ],
        in_specs=[hbm] * 8,
        out_specs=[vmem] * 7,
        scratch_shapes=[
            pltpu.VMEM((LROWS, nc * LCOLS), f32),
            pltpu.VMEM((nc, 40, 128), f32),
            pltpu.VMEM((nc, 16, 128), f32),
            pltpu.VMEM((BANDS, 64, 128), f32),
            pltpu.VMEM((BANDS, 16, 128), f32),
            pltpu.VMEM((2, PAN_RIM, COLS), f32),
            pltpu.VMEM((2, PAN_RIM, COLS), f32),
            pltpu.VMEM((2, 64, 128), f32),
            pltpu.VMEM((2, 64, 128), f32),
            pltpu.VMEM((2, 2, 16, 128), f32),
            pltpu.VMEM((2, 2, 16, 128), f32),
            *[pltpu.VMEM(table.shape, bf16) for table in tables[2:]],
            pltpu.VMEM((2, PAN_EXT, COLS + 128), bf16),
            pltpu.VMEM((3, 3 * PAN_EXT, COLS), bf16),
            pltpu.VMEM((BANDS * 32, 256), f32),
            pltpu.SMEM((3, BANDS), f32),
            pltpu.SemaphoreType.DMA((8,)),
            pltpu.SemaphoreType.DMA((3, 2)),
            pltpu.SemaphoreType.DMA((3,)),
            pltpu.SemaphoreType.DMA((6,)),
        ],
        compiler_params=pltpu.CompilerParams(
            collective_id=0, has_side_effects=True, vmem_limit_bytes=32 * 1024 * 1024
        ),
    )(in_hbm(ms), in_hbm(pan), in_hbm(gains.T), *[in_hbm(jnp.asarray(table)) for table in tables])
    return pl.pallas_call(
        functools.partial(finish, nc),
        out_shape=jax.ShapeDtypeStruct((BANDS, ROWS, COLS), f32),
        in_specs=[vmem] * 7,
        out_specs=hbm,
        scratch_shapes=[pltpu.VMEM((BANDS, ROWS, COLS), f32), pltpu.SemaphoreType.DMA],
        compiler_params=pltpu.CompilerParams(vmem_limit_bytes=16 * 1024 * 1024),
    )(*shared)


def solution(mesh):
    tables = make_tables()
    nr, nc = mesh.shape["row"], mesh.shape["col"]
    return jax.shard_map(
        functools.partial(on_device, nr, nc, tables),
        mesh=mesh,
        in_specs=(P("col", "row", None), P("row", "col"), P()),
        out_specs=P(None, "row", "col"),
        check_vma=False,
    )
```

```python
import functools
import math

import jax
import jax.numpy as jnp
import ml_dtypes
import numpy as np
from jax import lax
from jax.experimental import pallas as pl
from jax.experimental.pallas import tpu as pltpu
from jax.sharding import PartitionSpec as P

MESH = pl.DeviceIdType.MESH
BF16 = ml_dtypes.bfloat16

TAPS = [
    0.2303778133088964,
    0.7148465705529154,
    0.6308807679298587,
    -0.0279837694168599,
    -0.1870348117190931,
    0.0308413818355607,
    0.0328830116668852,
    -0.0105974017850690,
]

ROWS, COLS = 128, 512
LROWS, LCOLS = 32, 128
PAN_RIM = 32
PAN_SENT = 48
PAN_EXT = ROWS + 2 * PAN_RIM
MS_RIM = 16
BANDS = 8

RIM_PIECES = [(3 * j, 3, (0, 26 * j), 3, 29) for j in range(4)]
RIM_PIECES += [(12, 1, (0, 104), 3, 16), (12, 1, (1, 104), 16, 29)]


def windows(level):
    found = []
    for tree in range(2):
        taps = TAPS if tree == 0 else TAPS[::-1]
        cascade, shift = [1.0], 0
        for lev in range(level):
            longer = [0.0] * (len(cascade) + 7 * 2**lev)
            for i, value in enumerate(cascade):
                for j, tap in enumerate(taps):
                    longer[i + j * 2**lev] += value * tap
            cascade, shift = longer, shift + (3 + tree) * 2**lev
        found.append((2**level, shift, cascade))
    return found


def projection(level):
    rows = [{} for _ in range(8)]
    for step, shift, cascade in windows(level):
        for m in range(8):
            for k in range(-64, 64):
                at = m - step * k + shift
                if 0 <= at < len(cascade):
                    for i, value in enumerate(cascade):
                        offset = step * k - shift + i - m
                        rows[m][offset] = rows[m].get(offset, 0.0) + 0.5 * cascade[at] * value
    return rows


def cubic_weight(distance):
    magnitude = abs(distance)
    if magnitude <= 1.0:
        return 1.5 * magnitude**3 - 2.5 * magnitude**2 + 1.0
    if magnitude < 2.0:
        return -0.5 * magnitude**3 + 2.5 * magnitude**2 - 4.0 * magnitude + 2.0
    return 0.0


def upsampled_projection():
    rows = [{} for _ in range(8)]
    for m, weights in enumerate(projection(3)):
        for offset in sorted(weights):
            position = (m + offset + 0.5) / 4.0 - 0.5
            floor = math.floor(position)
            for low in range(floor - 1, floor + 3):
                term = weights[offset] * cubic_weight(position - low)
                rows[m][low] = rows[m].get(low, 0.0) + term
    return rows


def split_parts(matrix):
    high = matrix.astype(np.float32).astype(BF16)
    low = (matrix - high.astype(np.float64)).astype(np.float32).astype(BF16)
    return high, low


def pan_matrix(level, outs, ins, start):
    matrix = np.zeros((outs, ins))
    rows = projection(level)
    for m in range(outs):
        for offset, weight in rows[m % 8].items():
            if 0 <= m + offset - start < ins:
                matrix[m, m + offset - start] = weight
    return matrix


def straddling(edge):
    found = []
    for level in (1, 2, 3):
        for step, shift, cascade in windows(level):
            for k in range(-64, 128):
                first = step * k - shift
                if first < edge < first + len(cascade):
                    found.append((level, first, cascade))
    return found


def row_tables():
    above, below = straddling(0), straddling(ROWS)
    down = np.zeros((PAN_RIM, PAN_SENT))
    up = np.zeros((PAN_RIM, PAN_SENT))
    merged = np.zeros((3, ROWS, PAN_EXT))
    for level in (1, 2, 3):
        merged[level - 1, :, :ROWS] = pan_matrix(level, ROWS, ROWS, 0)
    for at, (level, first, cascade) in enumerate(above):
        for i, weight in enumerate(cascade):
            if first + i < 0:
                down[at, first + i + PAN_SENT] = weight
            else:
                merged[level - 1, first + i, ROWS + at] = 0.5 * weight
    for at, (level, first, cascade) in enumerate(below):
        for i, weight in enumerate(cascade):
            if first + i >= ROWS:
                up[at, first + i - ROWS] = weight
            else:
                merged[level - 1, first + i, ROWS + PAN_RIM + at] = 0.5 * weight
    return down, up, merged


def ms_matrix(outs, ins, lows):
    place = {low: at for at, low in lows}
    matrix = np.zeros((outs, ins))
    rows = upsampled_projection()
    for m in range(outs):
        for low, weight in rows[m % 8].items():
            matrix[m, place[low + 2 * (m // 8)]] = weight
    return matrix


def make_tables():
    ms_rows = []
    for odd in (0, 1):
        inner, outer = (-16, 32) if odd else (32, -13)
        lows = [(i, i) for i in range(LROWS)]
        lows += [(LROWS + i, inner + i) for i in range(16)]
        lows += [(LROWS + 19 + i, outer + i) for i in range(13)]
        high, low = split_parts(ms_matrix(ROWS, 64, lows))
        ms_rows.append(np.concatenate([high, high, low], 1))
    lows = [(i, i) for i in range(LCOLS)]
    lows += [(LCOLS + i, i - MS_RIM) for i in range(MS_RIM)]
    lows += [(LCOLS + MS_RIM + i, LCOLS + i) for i in range(MS_RIM)]
    high, low = split_parts(ms_matrix(COLS, 256, lows).T)
    ms_cols = np.concatenate([high, high, low], 0)
    matrix = np.concatenate([pan_matrix(level, 128, 256, -64) for level in (1, 2, 3)], 0).T
    high, low = split_parts(matrix)
    pan_cols = np.concatenate([high, high, low], 0)
    sums, pan_rows = [], []
    down, up, merged = row_tables()
    for matrix in (down, up):
        high, low = split_parts(matrix)
        sums.append(np.concatenate([high, high, low], 1))
    for level in range(3):
        high, low = split_parts(merged[level])
        pan_rows.append(np.concatenate([high, high, low], 1))
    return np.stack(ms_rows), ms_cols, pan_cols, np.stack(pan_rows), np.stack(sums)


def parts_of(x):
    high = x.astype(jnp.bfloat16)
    low = (x - high.astype(jnp.float32)).astype(jnp.bfloat16)
    return high, low


def rolled(tiles, beside):
    left = lax.broadcasted_iota(jnp.int32, beside.shape, 1) < 64
    turned = [pltpu.roll(tile, 64, 1) for tile in tiles]
    firsts, seconds = [beside] + turned, turned + [beside]
    return [jnp.where(left, one, two) for one, two in zip(firsts, seconds)]


def column_parts(x, ms_cols):
    high, low = parts_of(x)
    y = jnp.dot(
        jnp.concatenate([high, low, high], 1), ms_cols[...], preferred_element_type=jnp.float32
    )
    return parts_of(y)


def spread(
    nr, nc,
    ms_hbm, pan_hbm, gains_hbm, ms_rows_hbm, ms_cols_hbm, pan_cols_hbm, pan_rows_hbm, sums_hbm,
    details, weights, ysplit, xlast, ms_cols, ms_rows,
    ms_own, stage, ostage, mbuf, obuf, pan_own, psums, pan_above_below, pstage, precv, cstage, crecv,
    pan_cols, pan_rows, sums,
    pan_split, zbuf, xbuf,
    gains, load_sems, ms_recv, pan_recv, send_sems,
):
    r, c = lax.axis_index("row"), lax.axis_index("col")
    half = nc // 2
    row_of = {d: lax.rem(r + d + nr, nr) for d in (-1, 0, 1)}
    side, place = c // half, lax.rem(c, half)
    halves = [lax.rem(side + a, 2) * half for a in range(2)]
    col_of = {
        (a, k): halves[a] + lax.rem(place + k, half) for a in range(2) for k in range(half)
    }

    ms_load = pltpu.make_async_copy(ms_hbm.at[0], ms_own, load_sems.at[0])
    pan_load = pltpu.make_async_copy(pan_hbm, pan_own, load_sems.at[1])
    sums_load = pltpu.make_async_copy(sums_hbm, sums, load_sems.at[7])

    odd = lax.rem(r, 2)
    inner = lax.rem(r + 1 - 2 * odd + nr, nr)
    outer = lax.rem(r - 1 + 2 * odd + nr, nr)

    barrier = pltpu.get_barrier_semaphore()
    for col in col_of.values():
        pl.semaphore_signal(barrier, inc=1, device_id=(outer, col), device_id_type=MESH)
    for at, col in col_of.items():
        if at != (0, 0):
            pl.semaphore_signal(barrier, inc=1, device_id=(r, col), device_id_type=MESH)
    for k in (0, 1, nc - 1):
        pl.semaphore_signal(
            barrier, inc=1, device_id=(inner, lax.rem(c + k, nc)), device_id_type=MESH
        )

    ms_load.start()
    pan_load.start()
    sums_load.start()
    table_loads = [
        pltpu.make_async_copy(source, target, load_sems.at[2 + i])
        for i, (source, target) in enumerate(
            (
                (pan_cols_hbm, pan_cols),
                (pan_rows_hbm, pan_rows),
                (gains_hbm, gains),
                (ms_cols_hbm, ms_cols),
                (ms_rows_hbm.at[odd], ms_rows),
            )
        )
    ]
    for load in table_loads:
        load.start()

    lane = lax.broadcasted_iota(jnp.int32, (8, 128), 1)
    sublane = lax.broadcasted_iota(jnp.int32, (8, 128), 0)

    ms_load.wait()
    for dest in range(nc):
        tile = slice(128 * dest, 128 * dest + 128)
        before = (dest - 1) % nc
        after = (dest + 1) % nc
        stage[dest, 0:16] = ms_own[0:16, tile]
        stage[dest, 24:40] = ms_own[16:32, tile]
        rim = None
        for q in range(4):
            rows = slice(8 * q, 8 * q + 8)
            both = jnp.where(
                lane < 64,
                ms_own[rows, 128 * after : 128 * after + 128],
                ms_own[rows, 128 * before : 128 * before + 128],
            )
            both = pltpu.roll(both, (16 + 32 * q) % 128, 1)
            rim = both if rim is None else jnp.where(lane < 32 * q, rim, both)
        stage[dest, 16:24] = rim

    for way in range(2):

        @pl.when(odd == way)
        def _():
            for dest in range(nc):
                tile = slice(128 * dest, 128 * dest + 128)
                if way:
                    upper, lower = ms_own[16:24, tile], ms_own[24:32, tile]
                else:
                    upper = pltpu.roll(ms_own[0:8, tile], 3, 0)
                    lower = jnp.where(sublane < 3, upper, pltpu.roll(ms_own[8:16, tile], 3, 0))
                rim = stage[dest, 16:24]
                for i, count, at, first, last in RIM_PIECES:
                    row = i + 19 * way
                    while count:
                        q, sub = row // 8, row % 8
                        now = min(count, 8 - sub)
                        moved = pltpu.roll(rim, (at[0] - sub) % 8, 0)
                        moved = pltpu.roll(moved, (at[1] - 32 * q - first) % 128, 1)
                        inside = (sublane >= at[0]) & (sublane < at[0] + now)
                        inside &= (lane >= at[1]) & (lane < at[1] + last - first)
                        upper = jnp.where(inside, moved, upper)
                        row, count, at = row + now, count - now, (at[0] + now, at[1])
                ostage[dest, 0:8] = upper
                ostage[dest, 8:16] = lower

    pl.semaphore_wait(barrier, 2 * nc + 2)

    def remote(source, target, send_sem, recv_sem, row, col):
        return pltpu.make_async_remote_copy(
            src_ref=source,
            dst_ref=target,
            send_sem=send_sem,
            recv_sem=recv_sem,
            device_id=(row, col),
            device_id_type=MESH,
        )

    def rows_of(first, count):
        return pl.ds(pl.multiple_of(first, 8), count)

    for a in (1, 0):
        for k in range(half):
            if a or k:
                col = col_of[a, k]
                remote(
                    stage.at[col], mbuf.at[c, 0:40], send_sems.at[0], ms_recv.at[0, a], r, col
                ).start()
    mbuf[c, 0:40] = stage[c]

    pan_load.wait()
    sums_load.wait()
    for way, rows in ((0, slice(ROWS - PAN_SENT, ROWS)), (1, slice(0, PAN_SENT))):
        high, low = parts_of(pan_own[rows])
        psums[way] = jnp.dot(
            sums[way], jnp.concatenate([high, low, high], 0), preferred_element_type=jnp.float32
        )
    for source, at in ((pan_own, pstage), (psums.at[0], cstage.at[0]), (psums.at[1], cstage.at[1])):
        half_rows = source.shape[0] // 2
        left = lax.broadcasted_iota(jnp.int32, (half_rows, 128), 1) < 64
        last, first = source[:, 384:512], source[:, 0:128]
        at[0] = jnp.where(left, pltpu.roll(last[:half_rows], 64, 1), last[half_rows:])
        at[1] = jnp.where(left, first[:half_rows], pltpu.roll(first[half_rows:], 64, 1))

    def send_outer(a):
        for k in range(half):
            col = col_of[a, k]
            remote(
                ostage.at[col], obuf.at[c], send_sems.at[1], ms_recv.at[1, a], outer, col
            ).start()

    send_outer(1)
    for way, d in ((0, 1), (1, -1)):
        remote(
            psums.at[way], pan_above_below.at[way],
            send_sems.at[3], pan_recv.at[0], row_of[d], c,
        ).start()
    for side_at, k in ((0, 1), (1, nc - 1)):
        beside = lax.rem(c + k, nc)
        remote(
            pstage.at[side_at], precv.at[side_at], send_sems.at[4], pan_recv.at[1], r, beside
        ).start()
        for way, d in ((0, 1), (1, -1)):
            remote(
                cstage.at[way, side_at], crecv.at[way, side_at],
                send_sems.at[5], pan_recv.at[2], row_of[d], beside,
            ).start()
    send_outer(0)

    for a in (0, 1):
        arrived = mbuf.at[0 : half - 1 + a, 0:40]
        remote(arrived, arrived, send_sems.at[0], ms_recv.at[0, a], r, col_of[0, 1]).wait_recv()
        bands = pl.ds(halves[a], half)
        remote(
            mbuf.at[bands, rows_of(16 - 16 * odd, 24)], mbuf.at[bands, 40:64],
            send_sems.at[2], ms_recv.at[2, a], inner, c,
        ).start()

    def unpacked(packed):
        left = lax.broadcasted_iota(jnp.int32, packed.shape[1:], 1) < 64
        one, two = packed[0], packed[1]
        return jnp.concatenate(
            [
                jnp.where(left, one, pltpu.roll(two, 64, 1)),
                jnp.where(left, pltpu.roll(one, 64, 1), two),
            ],
            0,
        )

    def pan_columns(rows, count, tiles, ends):
        for t, tile in enumerate(rolled(tiles, ends)):
            for part, value in enumerate(parts_of(tile)):
                pan_split[part, rows : rows + count, 128 * t : 128 * t + 128] = value
        for j in range(4):
            window = slice(128 * j, 128 * j + 256)
            high, low = (pan_split[part, rows : rows + count, window] for part in range(2))
            z = jnp.dot(
                jnp.concatenate([high, low, high], 1),
                pan_cols[...],
                preferred_element_type=jnp.float32,
            )
            for level in range(3):
                high, low = parts_of(z[:, 128 * level : 128 * level + 128])
                for at, part in ((0, high), (1, low), (2, high)):
                    first = PAN_EXT * at + rows
                    zbuf[level, first : first + count, 128 * j : 128 * j + 128] = part

    def ms_columns(bands, at):
        high, low = column_parts(xbuf[0 : 32 * len(bands)], ms_cols)
        for i, b in enumerate(bands):
            ysplit[b, at : at + 32] = high[32 * i : 32 * i + 32]
            ysplit[b, 64 + at : 96 + at] = low[32 * i : 32 * i + 32]

    for b in range(BANDS):
        rim = mbuf[b, 16:24]
        for q, first in enumerate((0, 8, 24, 32)):
            rows = slice(32 * b + 8 * q, 32 * b + 8 * q + 8)
            xbuf[rows, 0:128] = mbuf[b, first : first + 8]
            xbuf[rows, 128:256] = pltpu.roll(rim, (128 - 32 * q) % 128, 1)
    for load in table_loads:
        load.wait()
    ms_columns(range(BANDS), 0)

    remote(pstage, precv, send_sems.at[4], pan_recv.at[1], r, col_of[0, 1]).wait_recv()
    tiles = [pan_own[:, 128 * t : 128 * t + 128] for t in range(4)]
    pan_columns(0, ROWS, tiles, unpacked(precv))
    remote(psums, psums, send_sems.at[3], pan_recv.at[0], row_of[1], c).wait_recv()
    remote(cstage, crecv, send_sems.at[5], pan_recv.at[2], row_of[1], c).wait_recv()
    tiles = [
        jnp.concatenate([pan_above_below[way, :, 128 * t : 128 * t + 128] for way in range(2)], 0)
        for t in range(4)
    ]
    ends = jnp.concatenate([unpacked(crecv.at[0]), unpacked(crecv.at[1])], 0)
    pan_columns(ROWS, 2 * PAN_RIM, tiles, ends)
    finer = pan_own[...]
    for level in range(3):
        coarser = jnp.dot(pan_rows[level], zbuf[level], preferred_element_type=jnp.float32)
        details[level] = finer - coarser
        finer = coarser

    for b in range(BANDS):
        for level in range(3):
            at = 3 * b + level
            weights[at : at + 1] = jnp.full((1, COLS), gains[level, b], jnp.float32)

    for a in range(2):
        arrived = mbuf.at[0:half, 0:24]
        remote(arrived, arrived, send_sems.at[2], ms_recv.at[2, a], inner, c).wait_recv()
        arrived = obuf.at[0:half]
        remote(arrived, arrived, send_sems.at[1], ms_recv.at[1, a], outer, c).wait_recv()
        bands = [halves[a] + k for k in range(half)]
        target = xlast if a else xbuf
        for k, b in enumerate(bands):
            rim = mbuf[b, rows_of(56 - 16 * odd, 8)]
            for q in range(2):
                rows = slice(32 * k + 8 * q, 32 * k + 8 * q + 8)
                target[rows, 0:128] = mbuf[b, rows_of(40 + 8 * odd + 8 * q, 8)]
                at = 32 * q + 64 * odd
                target[rows, 128:256] = pltpu.roll(rim, lax.rem(128 - at, 128), 1)
            upper, lower = obuf[b, 0:8], obuf[b, 8:16]
            rims = [upper, lower]
            for i, count, at, first, last in RIM_PIECES:
                moved = pltpu.roll(upper, (i + 3 - at[0]) % 8, 0)
                moved = pltpu.roll(moved, (first - at[1]) % 128, 1)
                for v in range(2):
                    low, high = i + 3 - 8 * v, i + 3 + count - 8 * v
                    if low < 8 and high > 0:
                        inside = (sublane >= low) & (sublane < high)
                        if last - first < 26:
                            inside &= (lane >= first) & (lane < last)
                        rims[v] = jnp.where(inside, moved, rims[v])
            for v, main in enumerate((upper, lower)):
                rows = slice(32 * k + 16 + 8 * v, 32 * k + 24 + 8 * v)
                target[rows, 0:128] = main
                target[rows, 128:256] = rims[v]
        if a == 0:
            ms_columns(bands, 32)

    sent = (stage.at[0 : nc - 1], ostage, mbuf.at[:, 0:24], psums, pstage, cstage)
    for at, source in enumerate(sent):
        remote(source, source, send_sems.at[at], pan_recv.at[0], inner, c).wait_send()


def finish(nc, details, weights, ysplit, xlast, ms_cols, ms_rows, out_hbm, result, sem):
    half = nc // 2
    side = lax.axis_index("col") // half
    for a in range(2):
        first = lax.rem(side + a, 2) * half
        if a:
            rim_high, rim_low = column_parts(xlast[...], ms_cols)
        for k in range(half):
            b = first + k
            if a:
                rows = slice(32 * k, 32 * k + 32)
                high = jnp.concatenate([ysplit[b, 0:32], rim_high[rows]], 0)
                low = jnp.concatenate([ysplit[b, 64:96], rim_low[rows]], 0)
            else:
                high, low = ysplit[b, 0:64], ysplit[b, 64:128]
            total = jnp.dot(
                ms_rows[...],
                jnp.concatenate([high, low, high], 0),
                preferred_element_type=jnp.float32,
            )
            for level in range(3):
                total += weights[pl.ds(3 * b + level, 1)] * details[level]
            result[b] = total
            for part in range(2):
                rows = pl.ds(64 * part, 64)
                pltpu.make_async_copy(result.at[b, rows], out_hbm.at[b, rows], sem).start()
    pltpu.make_async_copy(result, out_hbm, sem).wait()


def in_hbm(x):
    return pltpu.with_memory_space_constraint(x, pltpu.HBM)


def on_device(nr, nc, tables, ms, pan, gains):
    f32 = jnp.float32
    bf16 = jnp.bfloat16
    hbm = pl.BlockSpec(memory_space=pl.ANY)
    vmem = pl.BlockSpec(memory_space=pltpu.VMEM)
    shared = pl.pallas_call(
        functools.partial(spread, nr, nc),
        out_shape=[
            pltpu.VMEM((3, ROWS, COLS), f32),
            pltpu.VMEM((3 * BANDS, COLS), f32),
            pltpu.VMEM((BANDS, 128, COLS), bf16),
            pltpu.VMEM((BANDS // 2 * 32, 256), f32),
            pltpu.VMEM(tables[1].shape, bf16),
            pltpu.VMEM(tables[0].shape[1:], bf16),
        ],
        in_specs=[hbm] * 8,
        out_specs=[vmem] * 6,
        scratch_shapes=[
            pltpu.VMEM((LROWS, nc * LCOLS), f32),
            pltpu.VMEM((nc, 40, 128), f32),
            pltpu.VMEM((nc, 16, 128), f32),
            pltpu.VMEM((BANDS, 64, 128), f32),
            pltpu.VMEM((BANDS, 16, 128), f32),
            pltpu.VMEM((ROWS, COLS), f32),
            pltpu.VMEM((2, PAN_RIM, COLS), f32),
            pltpu.VMEM((2, PAN_RIM, COLS), f32),
            pltpu.VMEM((2, 64, 128), f32),
            pltpu.VMEM((2, 64, 128), f32),
            pltpu.VMEM((2, 2, 16, 128), f32),
            pltpu.VMEM((2, 2, 16, 128), f32),
            *[pltpu.VMEM(table.shape, bf16) for table in tables[2:]],
            pltpu.VMEM((2, PAN_EXT, COLS + 128), bf16),
            pltpu.VMEM((3, 3 * PAN_EXT, COLS), bf16),
            pltpu.VMEM((BANDS * 32, 256), f32),
            pltpu.SMEM((3, BANDS), f32),
            pltpu.SemaphoreType.DMA((8,)),
            pltpu.SemaphoreType.DMA((3, 2)),
            pltpu.SemaphoreType.DMA((3,)),
            pltpu.SemaphoreType.DMA((6,)),
        ],
        compiler_params=pltpu.CompilerParams(
            collective_id=0, has_side_effects=True, vmem_limit_bytes=32 * 1024 * 1024
        ),
    )(in_hbm(ms), in_hbm(pan), in_hbm(gains.T), *[in_hbm(jnp.asarray(table)) for table in tables])
    return pl.pallas_call(
        functools.partial(finish, nc),
        out_shape=jax.ShapeDtypeStruct((BANDS, ROWS, COLS), f32),
        in_specs=[vmem] * 6,
        out_specs=hbm,
        scratch_shapes=[pltpu.VMEM((BANDS, ROWS, COLS), f32), pltpu.SemaphoreType.DMA],
        compiler_params=pltpu.CompilerParams(vmem_limit_bytes=16 * 1024 * 1024),
    )(*shared)


def solution(mesh):
    tables = make_tables()
    nr, nc = mesh.shape["row"], mesh.shape["col"]
    return jax.shard_map(
        functools.partial(on_device, nr, nc, tables),
        mesh=mesh,
        in_specs=(P("col", "row", None), P("row", "col"), P()),
        out_specs=P(None, "row", "col"),
        check_vma=False,
    )
```

```python
import functools
import math

import jax
import jax.numpy as jnp
import ml_dtypes
import numpy as np
from jax import lax
from jax.experimental import pallas as pl
from jax.experimental.pallas import tpu as pltpu
from jax.sharding import PartitionSpec as P

MESH = pl.DeviceIdType.MESH
BF16 = ml_dtypes.bfloat16

TAPS = [
    0.2303778133088964,
    0.7148465705529154,
    0.6308807679298587,
    -0.0279837694168599,
    -0.1870348117190931,
    0.0308413818355607,
    0.0328830116668852,
    -0.0105974017850690,
]

ROWS, COLS = 128, 512
LROWS, LCOLS = 32, 128
PAN_RIM = 32
PAN_SENT = 48
PAN_EXT = ROWS + 2 * PAN_RIM
MS_RIM = 16
BANDS = 8

RIM_PIECES = [(3 * j, 3, (0, 26 * j), 3, 29) for j in range(4)]
RIM_PIECES += [(12, 1, (0, 104), 3, 16), (12, 1, (1, 104), 16, 29)]


def windows(level):
    found = []
    for tree in range(2):
        taps = TAPS if tree == 0 else TAPS[::-1]
        cascade, shift = [1.0], 0
        for lev in range(level):
            longer = [0.0] * (len(cascade) + 7 * 2**lev)
            for i, value in enumerate(cascade):
                for j, tap in enumerate(taps):
                    longer[i + j * 2**lev] += value * tap
            cascade, shift = longer, shift + (3 + tree) * 2**lev
        found.append((2**level, shift, cascade))
    return found


def projection(level):
    rows = [{} for _ in range(8)]
    for step, shift, cascade in windows(level):
        for m in range(8):
            for k in range(-64, 64):
                at = m - step * k + shift
                if 0 <= at < len(cascade):
                    for i, value in enumerate(cascade):
                        offset = step * k - shift + i - m
                        rows[m][offset] = rows[m].get(offset, 0.0) + 0.5 * cascade[at] * value
    return rows


def cubic_weight(distance):
    magnitude = abs(distance)
    if magnitude <= 1.0:
        return 1.5 * magnitude**3 - 2.5 * magnitude**2 + 1.0
    if magnitude < 2.0:
        return -0.5 * magnitude**3 + 2.5 * magnitude**2 - 4.0 * magnitude + 2.0
    return 0.0


def upsampled_projection():
    rows = [{} for _ in range(8)]
    for m, weights in enumerate(projection(3)):
        for offset in sorted(weights):
            position = (m + offset + 0.5) / 4.0 - 0.5
            floor = math.floor(position)
            for low in range(floor - 1, floor + 3):
                term = weights[offset] * cubic_weight(position - low)
                rows[m][low] = rows[m].get(low, 0.0) + term
    return rows


def split_parts(matrix):
    high = matrix.astype(np.float32).astype(BF16)
    low = (matrix - high.astype(np.float64)).astype(np.float32).astype(BF16)
    return high, low


def pan_matrix(level, outs, ins, start):
    matrix = np.zeros((outs, ins))
    rows = projection(level)
    for m in range(outs):
        for offset, weight in rows[m % 8].items():
            if 0 <= m + offset - start < ins:
                matrix[m, m + offset - start] = weight
    return matrix


def straddling(edge):
    found = []
    for level in (1, 2, 3):
        for step, shift, cascade in windows(level):
            for k in range(-64, 128):
                first = step * k - shift
                if first < edge < first + len(cascade):
                    found.append((level, first, cascade))
    return found


def row_tables():
    above, below = straddling(0), straddling(ROWS)
    down = np.zeros((PAN_RIM, PAN_SENT))
    up = np.zeros((PAN_RIM, PAN_SENT))
    merged = np.zeros((3, ROWS, PAN_EXT))
    for level in (1, 2, 3):
        merged[level - 1, :, :ROWS] = pan_matrix(level, ROWS, ROWS, 0)
    for at, (level, first, cascade) in enumerate(above):
        for i, weight in enumerate(cascade):
            if first + i < 0:
                down[at, first + i + PAN_SENT] = weight
            else:
                merged[level - 1, first + i, ROWS + at] = 0.5 * weight
    for at, (level, first, cascade) in enumerate(below):
        for i, weight in enumerate(cascade):
            if first + i >= ROWS:
                up[at, first + i - ROWS] = weight
            else:
                merged[level - 1, first + i, ROWS + PAN_RIM + at] = 0.5 * weight
    return down, up, merged


def ms_matrix(outs, ins, lows):
    place = {low: at for at, low in lows}
    matrix = np.zeros((outs, ins))
    rows = upsampled_projection()
    for m in range(outs):
        for low, weight in rows[m % 8].items():
            matrix[m, place[low + 2 * (m // 8)]] = weight
    return matrix


def make_tables():
    ms_rows = []
    for odd in (0, 1):
        inner, outer = (-16, 32) if odd else (32, -13)
        lows = [(i, i) for i in range(LROWS)]
        lows += [(LROWS + i, inner + i) for i in range(16)]
        lows += [(LROWS + 19 + i, outer + i) for i in range(13)]
        high, low = split_parts(ms_matrix(ROWS, 64, lows))
        ms_rows.append(np.concatenate([high, high, low], 1))
    lows = [(i, i) for i in range(LCOLS)]
    lows += [(LCOLS + i, i - MS_RIM) for i in range(MS_RIM)]
    lows += [(LCOLS + MS_RIM + i, LCOLS + i) for i in range(MS_RIM)]
    high, low = split_parts(ms_matrix(COLS, 256, lows).T)
    ms_cols = np.concatenate([high, high, low], 0)
    matrix = np.concatenate([pan_matrix(level, 128, 256, -64) for level in (1, 2, 3)], 0).T
    high, low = split_parts(matrix)
    pan_cols = np.concatenate([high, high, low], 0)
    sums, pan_rows = [], []
    down, up, merged = row_tables()
    for matrix in (down, up):
        high, low = split_parts(matrix)
        sums.append(np.concatenate([high, high, low], 1))
    for level in range(3):
        high, low = split_parts(merged[level])
        pan_rows.append(np.concatenate([high, high, low], 1))
    return np.stack(ms_rows), ms_cols, pan_cols, np.stack(pan_rows), np.stack(sums)


def parts_of(x):
    high = x.astype(jnp.bfloat16)
    low = (x - high.astype(jnp.float32)).astype(jnp.bfloat16)
    return high, low


def rolled(tiles, beside):
    left = lax.broadcasted_iota(jnp.int32, beside.shape, 1) < 64
    turned = [pltpu.roll(tile, 64, 1) for tile in tiles]
    firsts, seconds = [beside] + turned, turned + [beside]
    return [jnp.where(left, one, two) for one, two in zip(firsts, seconds)]


def column_parts(x, ms_cols):
    high, low = parts_of(x)
    y = jnp.dot(
        jnp.concatenate([high, low, high], 1), ms_cols[...], preferred_element_type=jnp.float32
    )
    return parts_of(y)


def spread(
    nr, nc,
    ms_hbm, pan_hbm, gains_hbm, ms_rows_hbm, ms_cols_hbm, pan_cols_hbm, pan_rows_hbm, sums_hbm,
    details, weights, ysplit, xlast, ms_cols, ms_rows,
    ms_own, stage, ostage, mbuf, obuf, pan_own, psums, pan_above_below, pstage, precv, cstage, crecv,
    pan_cols, pan_rows, sums,
    pan_split, zbuf, xbuf,
    gains, load_sems, ms_recv, pan_recv, send_sems,
):
    r, c = lax.axis_index("row"), lax.axis_index("col")
    half = nc // 2
    row_of = {d: lax.rem(r + d + nr, nr) for d in (-1, 0, 1)}
    side, place = c // half, lax.rem(c, half)
    halves = [lax.rem(side + a, 2) * half for a in range(2)]
    col_of = {
        (a, k): halves[a] + lax.rem(place + k, half) for a in range(2) for k in range(half)
    }

    ms_load = pltpu.make_async_copy(ms_hbm.at[0], ms_own, load_sems.at[0])
    pan_load = pltpu.make_async_copy(pan_hbm, pan_own, load_sems.at[1])
    sums_load = pltpu.make_async_copy(sums_hbm, sums, load_sems.at[7])

    odd = lax.rem(r, 2)
    inner = lax.rem(r + 1 - 2 * odd + nr, nr)
    outer = lax.rem(r - 1 + 2 * odd + nr, nr)

    barrier = pltpu.get_barrier_semaphore()
    for col in col_of.values():
        pl.semaphore_signal(barrier, inc=1, device_id=(outer, col), device_id_type=MESH)
    for at, col in col_of.items():
        if at != (0, 0):
            pl.semaphore_signal(barrier, inc=1, device_id=(r, col), device_id_type=MESH)
    for k in (0, 1, nc - 1):
        pl.semaphore_signal(
            barrier, inc=1, device_id=(inner, lax.rem(c + k, nc)), device_id_type=MESH
        )

    ms_load.start()
    pan_load.start()
    sums_load.start()
    table_loads = [
        pltpu.make_async_copy(source, target, load_sems.at[2 + i])
        for i, (source, target) in enumerate(
            (
                (pan_cols_hbm, pan_cols),
                (pan_rows_hbm, pan_rows),
                (gains_hbm, gains),
                (ms_cols_hbm, ms_cols),
                (ms_rows_hbm.at[odd], ms_rows),
            )
        )
    ]
    for load in table_loads:
        load.start()

    lane = lax.broadcasted_iota(jnp.int32, (8, 128), 1)
    sublane = lax.broadcasted_iota(jnp.int32, (8, 128), 0)

    ms_load.wait()
    for dest in range(nc):
        tile = slice(128 * dest, 128 * dest + 128)
        before = (dest - 1) % nc
        after = (dest + 1) % nc
        stage[dest, 0:16] = ms_own[0:16, tile]
        stage[dest, 24:40] = ms_own[16:32, tile]
        rim = None
        for q in range(4):
            rows = slice(8 * q, 8 * q + 8)
            both = jnp.where(
                lane < 64,
                ms_own[rows, 128 * after : 128 * after + 128],
                ms_own[rows, 128 * before : 128 * before + 128],
            )
            both = pltpu.roll(both, (16 + 32 * q) % 128, 1)
            rim = both if rim is None else jnp.where(lane < 32 * q, rim, both)
        stage[dest, 16:24] = rim

    for way in range(2):

        @pl.when(odd == way)
        def _():
            for dest in range(nc):
                tile = slice(128 * dest, 128 * dest + 128)
                if way:
                    upper, lower = ms_own[16:24, tile], ms_own[24:32, tile]
                else:
                    upper = pltpu.roll(ms_own[0:8, tile], 3, 0)
                    lower = jnp.where(sublane < 3, upper, pltpu.roll(ms_own[8:16, tile], 3, 0))
                rim = stage[dest, 16:24]
                for i, count, at, first, last in RIM_PIECES:
                    row = i + 19 * way
                    while count:
                        q, sub = row // 8, row % 8
                        now = min(count, 8 - sub)
                        moved = pltpu.roll(rim, (at[0] - sub) % 8, 0)
                        moved = pltpu.roll(moved, (at[1] - 32 * q - first) % 128, 1)
                        inside = (sublane >= at[0]) & (sublane < at[0] + now)
                        inside &= (lane >= at[1]) & (lane < at[1] + last - first)
                        upper = jnp.where(inside, moved, upper)
                        row, count, at = row + now, count - now, (at[0] + now, at[1])
                ostage[dest, 0:8] = upper
                ostage[dest, 8:16] = lower

    pl.semaphore_wait(barrier, 2 * nc + 2)

    def remote(source, target, send_sem, recv_sem, row, col):
        return pltpu.make_async_remote_copy(
            src_ref=source,
            dst_ref=target,
            send_sem=send_sem,
            recv_sem=recv_sem,
            device_id=(row, col),
            device_id_type=MESH,
        )

    def rows_of(first, count):
        return pl.ds(pl.multiple_of(first, 8), count)

    for a in (1, 0):
        for k in range(half):
            if a or k:
                col = col_of[a, k]
                remote(
                    stage.at[col], mbuf.at[c, 0:40], send_sems.at[0], ms_recv.at[0, a], r, col
                ).start()
    mbuf[c, 0:40] = stage[c]

    pan_load.wait()
    sums_load.wait()
    for way, rows in ((0, slice(ROWS - PAN_SENT, ROWS)), (1, slice(0, PAN_SENT))):
        high, low = parts_of(pan_own[rows])
        psums[way] = jnp.dot(
            sums[way], jnp.concatenate([high, low, high], 0), preferred_element_type=jnp.float32
        )
    for source, at in ((pan_own, pstage), (psums.at[0], cstage.at[0]), (psums.at[1], cstage.at[1])):
        half_rows = source.shape[0] // 2
        left = lax.broadcasted_iota(jnp.int32, (half_rows, 128), 1) < 64
        last, first = source[:, 384:512], source[:, 0:128]
        at[0] = jnp.where(left, pltpu.roll(last[:half_rows], 64, 1), last[half_rows:])
        at[1] = jnp.where(left, first[:half_rows], pltpu.roll(first[half_rows:], 64, 1))

    def send_outer(a):
        for k in range(half):
            col = col_of[a, k]
            remote(
                ostage.at[col], obuf.at[c], send_sems.at[1], ms_recv.at[1, a], outer, col
            ).start()

    send_outer(1)
    for way, d in ((0, 1), (1, -1)):
        remote(
            psums.at[way], pan_above_below.at[way],
            send_sems.at[3], pan_recv.at[0], row_of[d], c,
        ).start()
    for side_at, k in ((0, 1), (1, nc - 1)):
        beside = lax.rem(c + k, nc)
        remote(
            pstage.at[side_at], precv.at[side_at], send_sems.at[4], pan_recv.at[1], r, beside
        ).start()
        for way, d in ((0, 1), (1, -1)):
            remote(
                cstage.at[way, side_at], crecv.at[way, side_at],
                send_sems.at[5], pan_recv.at[2], row_of[d], beside,
            ).start()
    send_outer(0)

    for a in (0, 1):
        arrived = mbuf.at[0 : half - 1 + a, 0:40]
        remote(arrived, arrived, send_sems.at[0], ms_recv.at[0, a], r, col_of[0, 1]).wait_recv()
        bands = pl.ds(halves[a], half)
        remote(
            mbuf.at[bands, rows_of(16 - 16 * odd, 24)], mbuf.at[bands, 40:64],
            send_sems.at[2], ms_recv.at[2, a], inner, c,
        ).start()

    def unpacked(packed):
        left = lax.broadcasted_iota(jnp.int32, packed.shape[1:], 1) < 64
        one, two = packed[0], packed[1]
        return jnp.concatenate(
            [
                jnp.where(left, one, pltpu.roll(two, 64, 1)),
                jnp.where(left, pltpu.roll(one, 64, 1), two),
            ],
            0,
        )

    def pan_columns(rows, count, tiles, ends):
        for t, tile in enumerate(rolled(tiles, ends)):
            for part, value in enumerate(parts_of(tile)):
                pan_split[part, rows : rows + count, 128 * t : 128 * t + 128] = value
        for j in range(4):
            window = slice(128 * j, 128 * j + 256)
            high, low = (pan_split[part, rows : rows + count, window] for part in range(2))
            z = jnp.dot(
                jnp.concatenate([high, low, high], 1),
                pan_cols[...],
                preferred_element_type=jnp.float32,
            )
            for level in range(3):
                high, low = parts_of(z[:, 128 * level : 128 * level + 128])
                for at, part in ((0, high), (1, low), (2, high)):
                    first = PAN_EXT * at + rows
                    zbuf[level, first : first + count, 128 * j : 128 * j + 128] = part

    def ms_columns(bands, at):
        high, low = column_parts(xbuf[0 : 32 * len(bands)], ms_cols)
        for i, b in enumerate(bands):
            ysplit[b, at : at + 32] = high[32 * i : 32 * i + 32]
            ysplit[b, 64 + at : 96 + at] = low[32 * i : 32 * i + 32]

    for b in range(BANDS):
        rim = mbuf[b, 16:24]
        for q, first in enumerate((0, 8, 24, 32)):
            rows = slice(32 * b + 8 * q, 32 * b + 8 * q + 8)
            xbuf[rows, 0:128] = mbuf[b, first : first + 8]
            xbuf[rows, 128:256] = pltpu.roll(rim, (128 - 32 * q) % 128, 1)
    for load in table_loads:
        load.wait()
    ms_columns(range(BANDS), 0)

    remote(pstage, precv, send_sems.at[4], pan_recv.at[1], r, col_of[0, 1]).wait_recv()
    tiles = [pan_own[:, 128 * t : 128 * t + 128] for t in range(4)]
    pan_columns(0, ROWS, tiles, unpacked(precv))
    remote(psums, psums, send_sems.at[3], pan_recv.at[0], row_of[1], c).wait_recv()
    remote(cstage, crecv, send_sems.at[5], pan_recv.at[2], row_of[1], c).wait_recv()
    tiles = [
        jnp.concatenate([pan_above_below[way, :, 128 * t : 128 * t + 128] for way in range(2)], 0)
        for t in range(4)
    ]
    ends = jnp.concatenate([unpacked(crecv.at[0]), unpacked(crecv.at[1])], 0)
    pan_columns(ROWS, 2 * PAN_RIM, tiles, ends)
    finer = pan_own[...]
    for level in range(3):
        coarser = jnp.dot(pan_rows[level], zbuf[level], preferred_element_type=jnp.float32)
        details[level] = finer - coarser
        finer = coarser

    for b in range(BANDS):
        for level in range(3):
            at = 3 * b + level
            weights[at : at + 1] = jnp.full((1, COLS), gains[level, b], jnp.float32)

    for a in range(2):
        arrived = mbuf.at[0:half, 0:24]
        remote(arrived, arrived, send_sems.at[2], ms_recv.at[2, a], inner, c).wait_recv()
        arrived = obuf.at[0:half]
        remote(arrived, arrived, send_sems.at[1], ms_recv.at[1, a], outer, c).wait_recv()
        bands = [halves[a] + k for k in range(half)]
        target = xlast if a else xbuf
        for k, b in enumerate(bands):
            rim = mbuf[b, rows_of(56 - 16 * odd, 8)]
            for q in range(2):
                rows = slice(32 * k + 8 * q, 32 * k + 8 * q + 8)
                target[rows, 0:128] = mbuf[b, rows_of(40 + 8 * odd + 8 * q, 8)]
                at = 32 * q + 64 * odd
                target[rows, 128:256] = pltpu.roll(rim, lax.rem(128 - at, 128), 1)
            upper, lower = obuf[b, 0:8], obuf[b, 8:16]
            rims = [upper, lower]
            for i, count, at, first, last in RIM_PIECES:
                moved = pltpu.roll(upper, (i + 3 - at[0]) % 8, 0)
                moved = pltpu.roll(moved, (first - at[1]) % 128, 1)
                for v in range(2):
                    low, high = i + 3 - 8 * v, i + 3 + count - 8 * v
                    if low < 8 and high > 0:
                        inside = (sublane >= low) & (sublane < high)
                        if last - first < 26:
                            inside &= (lane >= first) & (lane < last)
                        rims[v] = jnp.where(inside, moved, rims[v])
            for v, main in enumerate((upper, lower)):
                rows = slice(32 * k + 16 + 8 * v, 32 * k + 24 + 8 * v)
                target[rows, 0:128] = main
                target[rows, 128:256] = rims[v]
        if a == 0:
            ms_columns(bands, 32)

    sent = (stage.at[0 : nc - 1], ostage, mbuf.at[:, 0:24], psums, pstage, cstage)
    for at, source in enumerate(sent):
        remote(source, source, send_sems.at[at], pan_recv.at[0], inner, c).wait_send()


def finish(nc, details, weights, ysplit, xlast, ms_cols, ms_rows, out_hbm, result, sem):
    half = nc // 2
    side = lax.axis_index("col") // half
    bands = [lax.rem(side + a, 2) * half + k for a in range(2) for k in range(half)]

    def product(i, rims):
        b = bands[i]
        if i < half:
            high, low = ysplit[b, 0:64], ysplit[b, 64:128]
        else:
            rows = slice(32 * (i - half), 32 * (i - half) + 32)
            high = jnp.concatenate([ysplit[b, 0:32], rims[0][rows]], 0)
            low = jnp.concatenate([ysplit[b, 64:96], rims[1][rows]], 0)
        return jnp.dot(
            ms_rows[...],
            jnp.concatenate([high, low, high], 0),
            preferred_element_type=jnp.float32,
        )

    rims = None
    following = None
    for i, b in enumerate(bands):
        total = product(i, rims) if following is None else following
        if i == half - 2:
            rims = column_parts(xlast[...], ms_cols)
        if 0 < i < BANDS - 1:
            following = product(i + 1, rims)
        for level in range(3):
            total += weights[pl.ds(3 * b + level, 1)] * details[level]
        result[b] = total
        for part in range(2):
            rows = pl.ds(64 * part, 64)
            pltpu.make_async_copy(result.at[b, rows], out_hbm.at[b, rows], sem).start()
    pltpu.make_async_copy(result, out_hbm, sem).wait()


def in_hbm(x):
    return pltpu.with_memory_space_constraint(x, pltpu.HBM)


def on_device(nr, nc, tables, ms, pan, gains):
    f32 = jnp.float32
    bf16 = jnp.bfloat16
    hbm = pl.BlockSpec(memory_space=pl.ANY)
    vmem = pl.BlockSpec(memory_space=pltpu.VMEM)
    shared = pl.pallas_call(
        functools.partial(spread, nr, nc),
        out_shape=[
            pltpu.VMEM((3, ROWS, COLS), f32),
            pltpu.VMEM((3 * BANDS, COLS), f32),
            pltpu.VMEM((BANDS, 128, COLS), bf16),
            pltpu.VMEM((BANDS // 2 * 32, 256), f32),
            pltpu.VMEM(tables[1].shape, bf16),
            pltpu.VMEM(tables[0].shape[1:], bf16),
        ],
        in_specs=[hbm] * 8,
        out_specs=[vmem] * 6,
        scratch_shapes=[
            pltpu.VMEM((LROWS, nc * LCOLS), f32),
            pltpu.VMEM((nc, 40, 128), f32),
            pltpu.VMEM((nc, 16, 128), f32),
            pltpu.VMEM((BANDS, 64, 128), f32),
            pltpu.VMEM((BANDS, 16, 128), f32),
            pltpu.VMEM((ROWS, COLS), f32),
            pltpu.VMEM((2, PAN_RIM, COLS), f32),
            pltpu.VMEM((2, PAN_RIM, COLS), f32),
            pltpu.VMEM((2, 64, 128), f32),
            pltpu.VMEM((2, 64, 128), f32),
            pltpu.VMEM((2, 2, 16, 128), f32),
            pltpu.VMEM((2, 2, 16, 128), f32),
            *[pltpu.VMEM(table.shape, bf16) for table in tables[2:]],
            pltpu.VMEM((2, PAN_EXT, COLS + 128), bf16),
            pltpu.VMEM((3, 3 * PAN_EXT, COLS), bf16),
            pltpu.VMEM((BANDS * 32, 256), f32),
            pltpu.SMEM((3, BANDS), f32),
            pltpu.SemaphoreType.DMA((8,)),
            pltpu.SemaphoreType.DMA((3, 2)),
            pltpu.SemaphoreType.DMA((3,)),
            pltpu.SemaphoreType.DMA((6,)),
        ],
        compiler_params=pltpu.CompilerParams(
            collective_id=0, has_side_effects=True, vmem_limit_bytes=32 * 1024 * 1024
        ),
    )(in_hbm(ms), in_hbm(pan), in_hbm(gains.T), *[in_hbm(jnp.asarray(table)) for table in tables])
    return pl.pallas_call(
        functools.partial(finish, nc),
        out_shape=jax.ShapeDtypeStruct((BANDS, ROWS, COLS), f32),
        in_specs=[vmem] * 6,
        out_specs=hbm,
        scratch_shapes=[pltpu.VMEM((BANDS, ROWS, COLS), f32), pltpu.SemaphoreType.DMA],
        compiler_params=pltpu.CompilerParams(vmem_limit_bytes=16 * 1024 * 1024),
    )(*shared)


def solution(mesh):
    tables = make_tables()
    nr, nc = mesh.shape["row"], mesh.shape["col"]
    return jax.shard_map(
        functools.partial(on_device, nr, nc, tables),
        mesh=mesh,
        in_specs=(P("col", "row", None), P("row", "col"), P()),
        out_specs=P(None, "row", "col"),
        check_vma=False,
    )
```

```python
import functools
import math

import jax
import jax.numpy as jnp
import ml_dtypes
import numpy as np
from jax import lax
from jax.experimental import pallas as pl
from jax.experimental.pallas import tpu as pltpu
from jax.sharding import PartitionSpec as P

MESH = pl.DeviceIdType.MESH
BF16 = ml_dtypes.bfloat16

TAPS = [
    0.2303778133088964,
    0.7148465705529154,
    0.6308807679298587,
    -0.0279837694168599,
    -0.1870348117190931,
    0.0308413818355607,
    0.0328830116668852,
    -0.0105974017850690,
]

ROWS, COLS = 128, 512
LROWS, LCOLS = 32, 128
PAN_RIM = 32
PAN_SENT = 48
PAN_EXT = ROWS + 2 * PAN_RIM
MS_RIM = 16
BANDS = 8

RIM_PIECES = [(3 * j, 3, (0, 26 * j), 3, 29) for j in range(4)]
RIM_PIECES += [(12, 1, (0, 104), 3, 16), (12, 1, (1, 104), 16, 29)]


def windows(level):
    found = []
    for tree in range(2):
        taps = TAPS if tree == 0 else TAPS[::-1]
        cascade, shift = [1.0], 0
        for lev in range(level):
            longer = [0.0] * (len(cascade) + 7 * 2**lev)
            for i, value in enumerate(cascade):
                for j, tap in enumerate(taps):
                    longer[i + j * 2**lev] += value * tap
            cascade, shift = longer, shift + (3 + tree) * 2**lev
        found.append((2**level, shift, cascade))
    return found


def projection(level):
    rows = [{} for _ in range(8)]
    for step, shift, cascade in windows(level):
        for m in range(8):
            for k in range(-64, 64):
                at = m - step * k + shift
                if 0 <= at < len(cascade):
                    for i, value in enumerate(cascade):
                        offset = step * k - shift + i - m
                        rows[m][offset] = rows[m].get(offset, 0.0) + 0.5 * cascade[at] * value
    return rows


def cubic_weight(distance):
    magnitude = abs(distance)
    if magnitude <= 1.0:
        return 1.5 * magnitude**3 - 2.5 * magnitude**2 + 1.0
    if magnitude < 2.0:
        return -0.5 * magnitude**3 + 2.5 * magnitude**2 - 4.0 * magnitude + 2.0
    return 0.0


def upsampled_projection():
    rows = [{} for _ in range(8)]
    for m, weights in enumerate(projection(3)):
        for offset in sorted(weights):
            position = (m + offset + 0.5) / 4.0 - 0.5
            floor = math.floor(position)
            for low in range(floor - 1, floor + 3):
                term = weights[offset] * cubic_weight(position - low)
                rows[m][low] = rows[m].get(low, 0.0) + term
    return rows


def split_parts(matrix):
    high = matrix.astype(np.float32).astype(BF16)
    low = (matrix - high.astype(np.float64)).astype(np.float32).astype(BF16)
    return high, low


def pan_matrix(level, outs, ins, start):
    matrix = np.zeros((outs, ins))
    rows = projection(level)
    for m in range(outs):
        for offset, weight in rows[m % 8].items():
            if 0 <= m + offset - start < ins:
                matrix[m, m + offset - start] = weight
    return matrix


def straddling(edge):
    found = []
    for level in (1, 2, 3):
        for step, shift, cascade in windows(level):
            for k in range(-64, 128):
                first = step * k - shift
                if first < edge < first + len(cascade):
                    found.append((level, first, cascade))
    return found


def row_tables():
    above, below = straddling(0), straddling(ROWS)
    down = np.zeros((PAN_RIM, PAN_SENT))
    up = np.zeros((PAN_RIM, PAN_SENT))
    merged = np.zeros((3, ROWS, PAN_EXT))
    for level in (1, 2, 3):
        merged[level - 1, :, :ROWS] = pan_matrix(level, ROWS, ROWS, 0)
    for at, (level, first, cascade) in enumerate(above):
        for i, weight in enumerate(cascade):
            if first + i < 0:
                down[at, first + i + PAN_SENT] = weight
            else:
                merged[level - 1, first + i, ROWS + at] = 0.5 * weight
    for at, (level, first, cascade) in enumerate(below):
        for i, weight in enumerate(cascade):
            if first + i >= ROWS:
                up[at, first + i - ROWS] = weight
            else:
                merged[level - 1, first + i, ROWS + PAN_RIM + at] = 0.5 * weight
    return down, up, merged


def ms_matrix(outs, ins, lows):
    place = {low: at for at, low in lows}
    matrix = np.zeros((outs, ins))
    rows = upsampled_projection()
    for m in range(outs):
        for low, weight in rows[m % 8].items():
            matrix[m, place[low + 2 * (m // 8)]] = weight
    return matrix


def make_tables():
    ms_rows = []
    for odd in (0, 1):
        inner, outer = (-16, 32) if odd else (32, -13)
        lows = [(i, i) for i in range(LROWS)]
        lows += [(LROWS + i, inner + i) for i in range(16)]
        lows += [(LROWS + 19 + i, outer + i) for i in range(13)]
        high, low = split_parts(ms_matrix(ROWS, 64, lows))
        ms_rows.append(np.concatenate([high, high, low], 1))
    lows = [(i, i) for i in range(LCOLS)]
    lows += [(LCOLS + i, i - MS_RIM) for i in range(MS_RIM)]
    lows += [(LCOLS + MS_RIM + i, LCOLS + i) for i in range(MS_RIM)]
    high, low = split_parts(ms_matrix(COLS, 256, lows).T)
    ms_cols = np.concatenate([high, high, low], 0)
    matrix = np.concatenate([pan_matrix(level, 128, 256, -64) for level in (1, 2, 3)], 0).T
    high, low = split_parts(matrix)
    pan_cols = np.concatenate([high, high, low], 0)
    sums, pan_rows = [], []
    down, up, merged = row_tables()
    for matrix in (down, up):
        high, low = split_parts(matrix)
        sums.append(np.concatenate([high, high, low], 1))
    for level in range(3):
        high, low = split_parts(merged[level])
        pan_rows.append(np.concatenate([high, high, low], 1))
    return np.stack(ms_rows), ms_cols, pan_cols, np.stack(pan_rows), np.stack(sums)


def parts_of(x):
    high = x.astype(jnp.bfloat16)
    low = (x - high.astype(jnp.float32)).astype(jnp.bfloat16)
    return high, low


def rolled(tiles, beside):
    left = lax.broadcasted_iota(jnp.int32, beside.shape, 1) < 64
    turned = [pltpu.roll(tile, 64, 1) for tile in tiles]
    firsts, seconds = [beside] + turned, turned + [beside]
    return [jnp.where(left, one, two) for one, two in zip(firsts, seconds)]


def column_parts(x, ms_cols):
    high, low = parts_of(x)
    y = jnp.dot(
        jnp.concatenate([high, low, high], 1), ms_cols[...], preferred_element_type=jnp.float32
    )
    return parts_of(y)


def spread(
    nr, nc,
    ms_hbm, pan_hbm, gains_hbm, ms_rows_hbm, ms_cols_hbm, pan_cols_hbm, pan_rows_hbm, sums_hbm,
    details, weights, ysplit, xlast, ms_cols, ms_rows,
    ms_own, stage, ostage, mbuf, obuf, pan_own, psums, pan_above_below, pstage, precv, cstage, crecv,
    pan_cols, pan_rows, sums,
    pan_split, zbuf, xbuf,
    gains, load_sems, ms_recv, pan_recv, send_sems,
):
    r, c = lax.axis_index("row"), lax.axis_index("col")
    half = nc // 2
    row_of = {d: lax.rem(r + d + nr, nr) for d in (-1, 0, 1)}
    side, place = c // half, lax.rem(c, half)
    halves = [lax.rem(side + a, 2) * half for a in range(2)]
    col_of = {
        (a, k): halves[a] + lax.rem(place + k, half) for a in range(2) for k in range(half)
    }

    ms_load = pltpu.make_async_copy(ms_hbm.at[0], ms_own, load_sems.at[0])
    pan_load = pltpu.make_async_copy(pan_hbm, pan_own, load_sems.at[1])
    sums_load = pltpu.make_async_copy(sums_hbm, sums, load_sems.at[7])

    odd = lax.rem(r, 2)
    inner = lax.rem(r + 1 - 2 * odd + nr, nr)
    outer = lax.rem(r - 1 + 2 * odd + nr, nr)

    barrier = pltpu.get_barrier_semaphore()
    for col in col_of.values():
        pl.semaphore_signal(barrier, inc=1, device_id=(outer, col), device_id_type=MESH)
    for at, col in col_of.items():
        if at != (0, 0):
            pl.semaphore_signal(barrier, inc=1, device_id=(r, col), device_id_type=MESH)
    for k in (0, 1, nc - 1):
        pl.semaphore_signal(
            barrier, inc=1, device_id=(inner, lax.rem(c + k, nc)), device_id_type=MESH
        )

    ms_load.start()
    pan_load.start()
    sums_load.start()
    table_loads = [
        pltpu.make_async_copy(source, target, load_sems.at[2 + i])
        for i, (source, target) in enumerate(
            (
                (pan_cols_hbm, pan_cols),
                (pan_rows_hbm, pan_rows),
                (gains_hbm, gains),
                (ms_cols_hbm, ms_cols),
                (ms_rows_hbm.at[odd], ms_rows),
            )
        )
    ]
    for load in table_loads:
        load.start()

    lane = lax.broadcasted_iota(jnp.int32, (8, 128), 1)
    sublane = lax.broadcasted_iota(jnp.int32, (8, 128), 0)

    ms_load.wait()
    for dest in range(nc):
        tile = slice(128 * dest, 128 * dest + 128)
        before = (dest - 1) % nc
        after = (dest + 1) % nc
        stage[dest, 0:16] = ms_own[0:16, tile]
        stage[dest, 24:40] = ms_own[16:32, tile]
        rim = None
        for q in range(4):
            rows = slice(8 * q, 8 * q + 8)
            both = jnp.where(
                lane < 64,
                ms_own[rows, 128 * after : 128 * after + 128],
                ms_own[rows, 128 * before : 128 * before + 128],
            )
            both = pltpu.roll(both, (16 + 32 * q) % 128, 1)
            rim = both if rim is None else jnp.where(lane < 32 * q, rim, both)
        stage[dest, 16:24] = rim

    for way in range(2):

        @pl.when(odd == way)
        def _():
            for dest in range(nc):
                tile = slice(128 * dest, 128 * dest + 128)
                if way:
                    upper, lower = ms_own[16:24, tile], ms_own[24:32, tile]
                else:
                    upper = pltpu.roll(ms_own[0:8, tile], 3, 0)
                    lower = jnp.where(sublane < 3, upper, pltpu.roll(ms_own[8:16, tile], 3, 0))
                rim = stage[dest, 16:24]
                for i, count, at, first, last in RIM_PIECES:
                    row = i + 19 * way
                    while count:
                        q, sub = row // 8, row % 8
                        now = min(count, 8 - sub)
                        moved = pltpu.roll(rim, (at[0] - sub) % 8, 0)
                        moved = pltpu.roll(moved, (at[1] - 32 * q - first) % 128, 1)
                        inside = (sublane >= at[0]) & (sublane < at[0] + now)
                        inside &= (lane >= at[1]) & (lane < at[1] + last - first)
                        upper = jnp.where(inside, moved, upper)
                        row, count, at = row + now, count - now, (at[0] + now, at[1])
                ostage[dest, 0:8] = upper
                ostage[dest, 8:16] = lower

    pl.semaphore_wait(barrier, 2 * nc + 2)

    def remote(source, target, send_sem, recv_sem, row, col):
        return pltpu.make_async_remote_copy(
            src_ref=source,
            dst_ref=target,
            send_sem=send_sem,
            recv_sem=recv_sem,
            device_id=(row, col),
            device_id_type=MESH,
        )

    def rows_of(first, count):
        return pl.ds(pl.multiple_of(first, 8), count)

    for a in (1, 0):
        for k in range(half):
            if a or k:
                col = col_of[a, k]
                remote(
                    stage.at[col], mbuf.at[c, 0:40], send_sems.at[0], ms_recv.at[0, a], r, col
                ).start()
    mbuf[c, 0:40] = stage[c]

    pan_load.wait()
    sums_load.wait()
    for way, rows in ((0, slice(ROWS - PAN_SENT, ROWS)), (1, slice(0, PAN_SENT))):
        high, low = parts_of(pan_own[rows])
        psums[way] = jnp.dot(
            sums[way], jnp.concatenate([high, low, high], 0), preferred_element_type=jnp.float32
        )
    for source, at in ((pan_own, pstage), (psums.at[0], cstage.at[0]), (psums.at[1], cstage.at[1])):
        half_rows = source.shape[0] // 2
        left = lax.broadcasted_iota(jnp.int32, (half_rows, 128), 1) < 64
        last, first = source[:, 384:512], source[:, 0:128]
        at[0] = jnp.where(left, pltpu.roll(last[:half_rows], 64, 1), last[half_rows:])
        at[1] = jnp.where(left, first[:half_rows], pltpu.roll(first[half_rows:], 64, 1))

    def send_outer(a):
        for k in range(half):
            col = col_of[a, k]
            remote(
                ostage.at[col], obuf.at[c], send_sems.at[1], ms_recv.at[1, a], outer, col
            ).start()

    send_outer(1)
    for way, d in ((0, 1), (1, -1)):
        remote(
            psums.at[way], pan_above_below.at[way],
            send_sems.at[1], pan_recv.at[0], row_of[d], c,
        ).start()
    for side_at, k in ((0, 1), (1, nc - 1)):
        beside = lax.rem(c + k, nc)
        remote(
            pstage.at[side_at], precv.at[side_at], send_sems.at[1], pan_recv.at[1], r, beside
        ).start()
        for way, d in ((0, 1), (1, -1)):
            remote(
                cstage.at[way, side_at], crecv.at[way, side_at],
                send_sems.at[2], pan_recv.at[0], row_of[d], beside,
            ).start()
    send_outer(0)

    for a in (0, 1):
        arrived = mbuf.at[0 : half - 1 + a, 0:40]
        remote(arrived, arrived, send_sems.at[0], ms_recv.at[0, a], r, col_of[0, 1]).wait_recv()
        bands = pl.ds(halves[a], half)
        remote(
            mbuf.at[bands, rows_of(16 - 16 * odd, 24)], mbuf.at[bands, 40:64],
            send_sems.at[2], ms_recv.at[2, a], inner, c,
        ).start()

    def unpacked(packed):
        left = lax.broadcasted_iota(jnp.int32, packed.shape[1:], 1) < 64
        one, two = packed[0], packed[1]
        return jnp.concatenate(
            [
                jnp.where(left, one, pltpu.roll(two, 64, 1)),
                jnp.where(left, pltpu.roll(one, 64, 1), two),
            ],
            0,
        )

    def pan_columns(rows, count, tiles, ends):
        for t, tile in enumerate(rolled(tiles, ends)):
            for part, value in enumerate(parts_of(tile)):
                pan_split[part, rows : rows + count, 128 * t : 128 * t + 128] = value
        for j in range(4):
            window = slice(128 * j, 128 * j + 256)
            high, low = (pan_split[part, rows : rows + count, window] for part in range(2))
            z = jnp.dot(
                jnp.concatenate([high, low, high], 1),
                pan_cols[...],
                preferred_element_type=jnp.float32,
            )
            for level in range(3):
                high, low = parts_of(z[:, 128 * level : 128 * level + 128])
                for at, part in ((0, high), (1, low), (2, high)):
                    first = PAN_EXT * at + rows
                    zbuf[level, first : first + count, 128 * j : 128 * j + 128] = part

    def ms_columns(bands, at):
        high, low = column_parts(xbuf[0 : 32 * len(bands)], ms_cols)
        for i, b in enumerate(bands):
            ysplit[b, at : at + 32] = high[32 * i : 32 * i + 32]
            ysplit[b, 64 + at : 96 + at] = low[32 * i : 32 * i + 32]

    for b in range(BANDS):
        rim = mbuf[b, 16:24]
        for q, first in enumerate((0, 8, 24, 32)):
            rows = slice(32 * b + 8 * q, 32 * b + 8 * q + 8)
            xbuf[rows, 0:128] = mbuf[b, first : first + 8]
            xbuf[rows, 128:256] = pltpu.roll(rim, (128 - 32 * q) % 128, 1)
    for load in table_loads:
        load.wait()
    ms_columns(range(BANDS), 0)

    remote(pstage, precv, send_sems.at[1], pan_recv.at[1], r, col_of[0, 1]).wait_recv()
    tiles = [pan_own[:, 128 * t : 128 * t + 128] for t in range(4)]
    pan_columns(0, ROWS, tiles, unpacked(precv))
    arrived = mbuf.at[:, 0:40]
    remote(arrived, arrived, send_sems.at[1], pan_recv.at[0], row_of[1], c).wait_recv()
    tiles = [
        jnp.concatenate([pan_above_below[way, :, 128 * t : 128 * t + 128] for way in range(2)], 0)
        for t in range(4)
    ]
    ends = jnp.concatenate([unpacked(crecv.at[0]), unpacked(crecv.at[1])], 0)
    pan_columns(ROWS, 2 * PAN_RIM, tiles, ends)
    finer = pan_own[...]
    for level in range(3):
        coarser = jnp.dot(pan_rows[level], zbuf[level], preferred_element_type=jnp.float32)
        details[level] = finer - coarser
        finer = coarser

    for b in range(BANDS):
        for level in range(3):
            at = 3 * b + level
            weights[at : at + 1] = jnp.full((1, COLS), gains[level, b], jnp.float32)

    for a in range(2):
        arrived = mbuf.at[0:half, 0:24]
        remote(arrived, arrived, send_sems.at[2], ms_recv.at[2, a], inner, c).wait_recv()
        arrived = obuf.at[0:half]
        remote(arrived, arrived, send_sems.at[1], ms_recv.at[1, a], outer, c).wait_recv()
        bands = [halves[a] + k for k in range(half)]
        target = xlast if a else xbuf
        for k, b in enumerate(bands):
            rim = mbuf[b, rows_of(56 - 16 * odd, 8)]
            for q in range(2):
                rows = slice(32 * k + 8 * q, 32 * k + 8 * q + 8)
                target[rows, 0:128] = mbuf[b, rows_of(40 + 8 * odd + 8 * q, 8)]
                at = 32 * q + 64 * odd
                target[rows, 128:256] = pltpu.roll(rim, lax.rem(128 - at, 128), 1)
            upper, lower = obuf[b, 0:8], obuf[b, 8:16]
            rims = [upper, lower]
            for i, count, at, first, last in RIM_PIECES:
                moved = pltpu.roll(upper, (i + 3 - at[0]) % 8, 0)
                moved = pltpu.roll(moved, (first - at[1]) % 128, 1)
                for v in range(2):
                    low, high = i + 3 - 8 * v, i + 3 + count - 8 * v
                    if low < 8 and high > 0:
                        inside = (sublane >= low) & (sublane < high)
                        if last - first < 26:
                            inside &= (lane >= first) & (lane < last)
                        rims[v] = jnp.where(inside, moved, rims[v])
            for v, main in enumerate((upper, lower)):
                rows = slice(32 * k + 16 + 8 * v, 32 * k + 24 + 8 * v)
                target[rows, 0:128] = main
                target[rows, 128:256] = rims[v]
        if a == 0:
            ms_columns(bands, 32)

    sent = (stage.at[0 : nc - 1], pan_own, psums)
    for at, source in enumerate(sent):
        remote(source, source, send_sems.at[at], pan_recv.at[0], inner, c).wait_send()


def finish(nc, details, weights, ysplit, xlast, ms_cols, ms_rows, out_hbm, result, sem):
    half = nc // 2
    side = lax.axis_index("col") // half
    bands = [lax.rem(side + a, 2) * half + k for a in range(2) for k in range(half)]

    def product(i, rims):
        b = bands[i]
        if i < half:
            high, low = ysplit[b, 0:64], ysplit[b, 64:128]
        else:
            rows = slice(32 * (i - half), 32 * (i - half) + 32)
            high = jnp.concatenate([ysplit[b, 0:32], rims[0][rows]], 0)
            low = jnp.concatenate([ysplit[b, 64:96], rims[1][rows]], 0)
        return jnp.dot(
            ms_rows[...],
            jnp.concatenate([high, low, high], 0),
            preferred_element_type=jnp.float32,
        )

    rims = None
    following = None
    for i, b in enumerate(bands):
        total = product(i, rims) if following is None else following
        if i == half - 2:
            rims = column_parts(xlast[...], ms_cols)
        if 0 < i < BANDS - 1:
            following = product(i + 1, rims)
        for level in range(3):
            total += weights[pl.ds(3 * b + level, 1)] * details[level]
        result[b] = total
        for part in range(2):
            rows = pl.ds(64 * part, 64)
            pltpu.make_async_copy(result.at[b, rows], out_hbm.at[b, rows], sem).start()
    pltpu.make_async_copy(result, out_hbm, sem).wait()


def in_hbm(x):
    return pltpu.with_memory_space_constraint(x, pltpu.HBM)


def on_device(nr, nc, tables, ms, pan, gains):
    f32 = jnp.float32
    bf16 = jnp.bfloat16
    hbm = pl.BlockSpec(memory_space=pl.ANY)
    vmem = pl.BlockSpec(memory_space=pltpu.VMEM)
    shared = pl.pallas_call(
        functools.partial(spread, nr, nc),
        out_shape=[
            pltpu.VMEM((3, ROWS, COLS), f32),
            pltpu.VMEM((3 * BANDS, COLS), f32),
            pltpu.VMEM((BANDS, 128, COLS), bf16),
            pltpu.VMEM((BANDS // 2 * 32, 256), f32),
            pltpu.VMEM(tables[1].shape, bf16),
            pltpu.VMEM(tables[0].shape[1:], bf16),
        ],
        in_specs=[hbm] * 8,
        out_specs=[vmem] * 6,
        scratch_shapes=[
            pltpu.VMEM((LROWS, nc * LCOLS), f32),
            pltpu.VMEM((nc, 40, 128), f32),
            pltpu.VMEM((nc, 16, 128), f32),
            pltpu.VMEM((BANDS, 64, 128), f32),
            pltpu.VMEM((BANDS, 16, 128), f32),
            pltpu.VMEM((ROWS, COLS), f32),
            pltpu.VMEM((2, PAN_RIM, COLS), f32),
            pltpu.VMEM((2, PAN_RIM, COLS), f32),
            pltpu.VMEM((2, 64, 128), f32),
            pltpu.VMEM((2, 64, 128), f32),
            pltpu.VMEM((2, 2, 16, 128), f32),
            pltpu.VMEM((2, 2, 16, 128), f32),
            *[pltpu.VMEM(table.shape, bf16) for table in tables[2:]],
            pltpu.VMEM((2, PAN_EXT, COLS + 128), bf16),
            pltpu.VMEM((3, 3 * PAN_EXT, COLS), bf16),
            pltpu.VMEM((BANDS * 32, 256), f32),
            pltpu.SMEM((3, BANDS), f32),
            pltpu.SemaphoreType.DMA((8,)),
            pltpu.SemaphoreType.DMA((3, 2)),
            pltpu.SemaphoreType.DMA((2,)),
            pltpu.SemaphoreType.DMA((3,)),
        ],
        compiler_params=pltpu.CompilerParams(
            collective_id=0, has_side_effects=True, vmem_limit_bytes=32 * 1024 * 1024
        ),
    )(in_hbm(ms), in_hbm(pan), in_hbm(gains.T), *[in_hbm(jnp.asarray(table)) for table in tables])
    return pl.pallas_call(
        functools.partial(finish, nc),
        out_shape=jax.ShapeDtypeStruct((BANDS, ROWS, COLS), f32),
        in_specs=[vmem] * 6,
        out_specs=hbm,
        scratch_shapes=[pltpu.VMEM((BANDS, ROWS, COLS), f32), pltpu.SemaphoreType.DMA],
        compiler_params=pltpu.CompilerParams(vmem_limit_bytes=16 * 1024 * 1024),
    )(*shared)


def solution(mesh):
    tables = make_tables()
    nr, nc = mesh.shape["row"], mesh.shape["col"]
    return jax.shard_map(
        functools.partial(on_device, nr, nc, tables),
        mesh=mesh,
        in_specs=(P("col", "row", None), P("row", "col"), P()),
        out_specs=P(None, "row", "col"),
        check_vma=False,
    )
```
